32 devices in a mesh: row: 2 (over x), col: 8 (over z, core), dp: 2 (over y).
Axes of the slice: x: 2, y: 2, z: 4, core: 2. Of those that a mesh axis runs over, the one named last changes fastest.
Arguments:
- layer_input: bfloat16 [512, 12288], P(('dp', 'col'), 'row'), parts along dimension 0, may hold values from -6 to 6
- layer_norm_gain: float32 [12288], P('row'), may hold values from 0.1 to 1.9
- w_qkv: bfloat16 [12288, 18432], P('row', 'col'), may hold values from -16 to 16
- w_out: bfloat16 [6144, 12288], P('col', 'row'), may hold values from -0.078125 to 0.078125
- out_grad: bfloat16 [512, 12288], P(('dp', 'col'), 'row'), parts along dimension 0, may hold values from -6 to 6
Outputs:
- input_gradient: bfloat16 [512, 12288], P(('dp', 'col'), 'row'), parts along dimension 0
- gain_gradient: float32 [24576], P(('dp', 'row')), parts along dimension 0
- grad_wqkv: bfloat16 [24576, 18432], P(('dp', 'row'), 'col'), parts along dimension 0
- grad_wout: bfloat16 [12288, 12288], P(('dp', 'col'), 'row'), parts along dimension 0
The draws below stay inside these ranges and needn't reach their ends.
There are 2 independent parts, one for each index of `dp`. The reference program is written for one: setup_inputs(seed, part) draws one part's arguments, and reference() takes and returns one part's arrays. A program takes and returns all parts, laid end to end along the dimension named above; an argument that names none is the same for every part. Nothing has to cross between parts.
All inputs are finite; a program needn't handle non-finite values.
Results may differ from the reference program's by a relative error of at most 0.0098.
Values may be sent and summed in bfloat16 or wider, within the bound.
A program may use at most 128 MiB of HBM per device.

```python
import math
import jax
import jax.numpy as jnp
from jax import lax

D = 12288
HEADS = 48
HS = 128
TOKENS = 256


def draw_w_qkv(key, part):
    key = jax.random.fold_in(key, 11)
    base_key = jax.random.fold_in(key, 0)
    base = jax.random.truncated_normal(base_key, -6.0, 6.0, (D, HEADS, 3, HS), jnp.float32) * D ** (-0.5)
    return base.reshape(D, HEADS * 3 * HS).astype(jnp.bfloat16)


def steps_of(key, extent, pieces, least, high):
    def one(axis_at, blocks):
        steps = jax.random.uniform(jax.random.fold_in(jax.random.fold_in(key, 6), axis_at), (blocks,), jnp.float32, least / len(pieces), high / len(pieces))
        return jnp.repeat(jnp.exp(steps), extent[axis_at] // blocks).reshape((-1,) + (1,) * (len(extent) - axis_at - 1))

    level = one(*pieces[0])
    for cut in pieces[1:]:
        level = level * one(*cut)
    return level


def normal_values(stream_key, extent, width, most, cuts=(), kind=jnp.bfloat16):
    values = jax.random.normal(stream_key, extent, jnp.float32) * width
    if len(cuts) > 0:
        values = steps_of(stream_key, extent, cuts, -0.22, 0.18) * values
    return jnp.clip(values, min=-most, max=most).astype(kind)


def setup_inputs(seed: int = 0, part: int = 0) -> dict:
    key_of = jax.random.split(jax.random.key(seed), 6)
    part_splits = jax.random.split(jax.random.fold_in(key_of[5], part), 6)
    layer_input = normal_values(part_splits[0], (TOKENS, D), 1.0, 6.0, ((0, 8), (1, 2)))
    layer_norm_gain = jnp.clip(1.0 + 0.18 * jax.random.normal(key_of[1], (D,), jnp.float32), 0.1, 1.9)
    w_qkv = draw_w_qkv(jax.random.fold_in(key_of[5], 71), part)
    w_out = normal_values(key_of[3], (HEADS * HS, D), (HEADS * HS) ** -0.5, 0.078125, ((0, 8), (1, 2)))
    out_grad = normal_values(part_splits[4], (TOKENS, D), 1.0, 6.0, ((0, 8), (1, 2)))
    return dict(layer_input=layer_input, layer_norm_gain=layer_norm_gain, w_qkv=w_qkv, w_out=w_out, out_grad=out_grad)


EPS = 1e-05

def reference(layer_input, layer_norm_gain, w_qkv, w_out, out_grad):
    scale = 1.0 / math.sqrt(HS)
    input_float = layer_input.astype(jnp.float32)
    average = lax.optimization_barrier(jnp.mean(input_float, axis=1, keepdims=True))
    centered_input = input_float - average
    variance = lax.optimization_barrier(jnp.mean(centered_input * centered_input, axis=1, keepdims=True))
    inverse_deviation = lax.rsqrt(variance + EPS)
    standardized_input = centered_input * inverse_deviation
    normalized_output = (standardized_input * layer_norm_gain[None, :]).astype(jnp.bfloat16)
    qkv = jnp.dot(normalized_output, w_qkv, preferred_element_type=jnp.float32).astype(jnp.bfloat16)
    qkv = qkv.reshape(TOKENS, HEADS, 3, HS)
    heads_first = jnp.transpose(qkv, (1, 2, 0, 3))
    position = jnp.arange(TOKENS)
    allowed = position[None, :] <= position[:, None]

    def probs_of(query, keys):
        scores = jnp.dot(query, keys.T, preferred_element_type=jnp.float32) * scale
        scores = jnp.where(allowed, scores, -jnp.inf)
        highest = lax.optimization_barrier(jnp.max(scores, axis=1, keepdims=True))
        powers = jnp.exp(scores - highest)
        return powers / lax.optimization_barrier(jnp.sum(powers, axis=1, keepdims=True))

    def forward_head(block):
        probs = probs_of(block[0], block[1])
        return jnp.dot(probs.astype(jnp.bfloat16), block[2], preferred_element_type=jnp.float32).astype(jnp.bfloat16)
    context_heads = lax.map(forward_head, heads_first)
    context = jnp.transpose(context_heads, (1, 0, 2)).reshape(TOKENS, HEADS * HS)
    grad_wout = jnp.dot(context.T, out_grad, preferred_element_type=jnp.float32).astype(jnp.bfloat16)
    d_context = jnp.dot(out_grad, w_out.T, preferred_element_type=jnp.float32).astype(jnp.bfloat16)
    d_context_heads = jnp.transpose(d_context.reshape(TOKENS, HEADS, HS), (1, 0, 2))

    def backward_head(items):
        block, grad = items
        query, keys, values = (block[0], block[1], block[2])
        probs = probs_of(query, keys)
        probs_b = probs.astype(jnp.bfloat16)
        d_probs = jnp.dot(grad, values.T, preferred_element_type=jnp.float32)
        delta = lax.optimization_barrier(jnp.sum(probs * d_probs, axis=1, keepdims=True))
        d_scores = (probs * (d_probs - delta) * scale).astype(jnp.bfloat16)
        d_query = jnp.dot(d_scores, keys, preferred_element_type=jnp.float32).astype(jnp.bfloat16)
        d_keys = jnp.dot(d_scores.T, query, preferred_element_type=jnp.float32).astype(jnp.bfloat16)
        d_values = jnp.dot(probs_b.T, grad, preferred_element_type=jnp.float32).astype(jnp.bfloat16)
        return jnp.stack([d_query, d_keys, d_values], axis=0)
    d_heads = lax.map(backward_head, (heads_first, d_context_heads))
    d_qkv = jnp.transpose(d_heads, (2, 0, 1, 3)).reshape(TOKENS, 3 * HEADS * HS)
    grad_wqkv = jnp.dot(normalized_output.T, d_qkv, preferred_element_type=jnp.float32).astype(jnp.bfloat16)
    normalized_gradient = jnp.dot(d_qkv, w_qkv.T, preferred_element_type=jnp.float32)
    gain_gradient = lax.optimization_barrier(jnp.sum(normalized_gradient * standardized_input, axis=0))
    scaled_gradient = normalized_gradient * layer_norm_gain[None, :]
    first_term = lax.optimization_barrier(jnp.mean(scaled_gradient, axis=1, keepdims=True))
    second_term = lax.optimization_barrier(jnp.mean(scaled_gradient * standardized_input, axis=1, keepdims=True))
    input_gradient = (inverse_deviation * (scaled_gradient - first_term - standardized_input * second_term)).astype(jnp.bfloat16)
    return (input_gradient, gain_gradient, grad_wqkv, grad_wout)
```

```python
import functools
import math

import jax
import jax.numpy as jnp
from jax import lax
from jax.experimental import pallas as pl
from jax.experimental.pallas import tpu as pltpu
from jax.sharding import PartitionSpec as P

HS = 128


EPS = 1e-05


def shards(layer_input, layer_norm_gain, w_qkv, w_out, out_grad):
    rows_here, features_here = layer_input.shape
    col_count = lax.axis_size("col")
    row_count = lax.axis_size("row")
    tokens = rows_here * col_count
    tok_row = tokens // row_count
    feature_width = features_here * row_count
    heads_here = w_qkv.shape[1] // (3 * HS)
    scale = 1.0 / math.sqrt(HS)
    input_float = layer_input.astype(jnp.float32)
    average = lax.psum(jnp.sum(input_float, axis=1), "row") / feature_width
    centered_input = input_float - average[:, None]
    variance = lax.psum(jnp.sum(centered_input * centered_input, axis=1), "row") / feature_width
    inverse_deviation = lax.rsqrt(variance + EPS)
    standardized_input = centered_input * inverse_deviation[:, None]
    normalized_output = (standardized_input * layer_norm_gain[None, :]).astype(jnp.bfloat16)
    normed_all = lax.all_gather(normalized_output, "col", axis=0, tiled=True)
    first_query = lax.axis_index("row") * tok_row
    piece = normed_all
    owned = lax.psum_scatter(
        jnp.dot(piece, w_qkv, preferred_element_type=jnp.float32),
        "row",
        scatter_dimension=0,
        tiled=True,
    ).astype(jnp.bfloat16)
    owned = owned.reshape(tok_row, heads_here, 3, HS)
    query = owned[:, :, 0]
    key_value = lax.all_gather(owned[:, :, 1:], "row", axis=0, tiled=True)
    keys = key_value[:, :, 0]
    values = key_value[:, :, 1]
    query_pos = first_query + jnp.arange(tok_row)
    key_pos = jnp.arange(tokens)
    allowed = key_pos[None, :] <= query_pos[:, None]
    scores = jnp.einsum("qhe,khe->hqk", query, keys, preferred_element_type=jnp.float32) * scale
    scores = jnp.where(allowed[None], scores, -jnp.inf)
    highest = jnp.max(scores, axis=2, keepdims=True)
    powers = jnp.exp(scores - highest)
    totals = jnp.sum(powers, axis=2, keepdims=True)
    probs = powers / totals
    probs_b = probs.astype(jnp.bfloat16)
    context = jnp.einsum(
        "hqk,khe->qhe", probs_b, values, preferred_element_type=jnp.float32
    ).astype(jnp.bfloat16)
    context_all = lax.all_gather(
        context.reshape(tok_row, heads_here * HS), "row", axis=0, tiled=True
    )
    grad_all = lax.all_gather(out_grad, "col", axis=0, tiled=True)
    grad_wout = lax.dot_general(
        context_all, grad_all, (((0,), (0,)), ((), ())), preferred_element_type=jnp.float32
    ).astype(jnp.bfloat16)
    piece = grad_all
    d_context = lax.psum_scatter(
        lax.dot_general(piece, w_out, (((1,), (1,)), ((), ())), preferred_element_type=jnp.float32),
        "row",
        scatter_dimension=0,
        tiled=True,
    ).astype(jnp.bfloat16)
    d_context = d_context.reshape(tok_row, heads_here, HS)
    d_probs = jnp.einsum("qhe,khe->hqk", d_context, values, preferred_element_type=jnp.float32)
    delta = jnp.sum(probs * d_probs, axis=2, keepdims=True)
    d_scores = (probs * (d_probs - delta) * scale).astype(jnp.bfloat16)
    d_query = jnp.einsum("hqk,khe->qhe", d_scores, keys, preferred_element_type=jnp.float32).astype(
        jnp.bfloat16
    )
    d_keys = jnp.einsum("hqk,qhe->khe", d_scores, query, preferred_element_type=jnp.float32)
    d_values = jnp.einsum("hqk,qhe->khe", probs_b, d_context, preferred_element_type=jnp.float32)
    d_pairs = jnp.stack([d_keys, d_values], axis=2)
    pair_owned = lax.psum_scatter(d_pairs, "row", scatter_dimension=0, tiled=True).astype(
        jnp.bfloat16
    )
    owned_grad = jnp.concatenate([d_query[:, :, None], pair_owned], axis=2)
    owned_grad = owned_grad.reshape(tok_row, heads_here * 3 * HS)
    d_qkv_all = lax.all_gather(owned_grad, "row", axis=0, tiled=True)
    grad_wqkv = lax.dot_general(
        normed_all, d_qkv_all, (((0,), (0,)), ((), ())), preferred_element_type=jnp.float32
    ).astype(jnp.bfloat16)
    piece = d_qkv_all
    normalized_gradient = lax.psum_scatter(
        lax.dot_general(piece, w_qkv, (((1,), (1,)), ((), ())), preferred_element_type=jnp.float32),
        "col",
        scatter_dimension=0,
        tiled=True,
    )
    gain_gradient = lax.psum(jnp.sum(normalized_gradient * standardized_input, axis=0), "col")
    scaled_gradient = normalized_gradient * layer_norm_gain[None, :]
    first_term_sum, second_term_sum = lax.psum(
        (jnp.sum(scaled_gradient, axis=1), jnp.sum(scaled_gradient * standardized_input, axis=1)),
        "row",
    )
    input_gradient = inverse_deviation[:, None] * (
        scaled_gradient
        - first_term_sum[:, None] / feature_width
        - standardized_input * (second_term_sum[:, None] / feature_width)
    )
    return (input_gradient.astype(jnp.bfloat16), gain_gradient, grad_wqkv, grad_wout)

MESH = pl.DeviceIdType.MESH
F32 = jnp.float32
BF16 = jnp.bfloat16
NT = (((1,), (1,)), ((), ()))
TN = (((0,), (0,)), ((), ()))
NN = (((1,), (0,)), ((), ()))


def mm(a, b, dims=NN):
    return lax.dot_general(a, b, dims, preferred_element_type=F32)


def block_kernel(
    chips, x_ref, gain_ref, g_ref, wqkv_hbm, wout_hbm,
    dx_ref, dgain_ref, n_out, g_out, ctx_out, dqkv_out,
    wqkv, wout, nbuf, gbuf, xhat, rstd_buf, stat_send, stat_recv,
    q_send, q_recv, qkv, probs, ctx, dc_send, dc_recv, dctx, dqkv,
    acc, sib_send, sib_recv, z_send, z_recv, gg_send, gg_recv, total,
    w_sem, out_sem, stat_ss, stat_rs, ag_up, ag_down, ag_recv, sib_ss, sib_rs,
    q_ss, q_rs, c_ss, c_rs, dc_ss, dc_rs, dq_ss, dq_rs,
    ps_ss, ps_rs, rs_ss, rs_rs, gg_ss, gg_rs,
):
    row = lax.axis_index("row")
    col = lax.axis_index("col")
    dp = lax.axis_index("dp")
    z = col // 2
    core = col % 2
    rows, width = x_ref.shape
    tokens = nbuf.shape[0]
    own_heads = qkv.shape[0]
    scale = 1.0 / math.sqrt(HS)
    across = (1 - row, col, dp)
    sibling = (row, z * 2 + 1 - core, dp)
    above = (row, jnp.minimum(z + 1, chips - 1) * 2 + core, dp)
    below = (row, jnp.maximum(z - 1, 0) * 2 + core, dp)
    peers = 2 * chips

    barrier = pltpu.get_barrier_semaphore()
    pl.semaphore_signal(barrier, inc=1, device_id=across, device_id_type=MESH)
    for k in range(1, peers):
        pl.semaphore_signal(
            barrier, inc=1, device_id=(row, (col + k) % peers, dp), device_id_type=MESH
        )
    load_qkv = pltpu.make_async_copy(wqkv_hbm, wqkv, w_sem.at[0])
    load_out = pltpu.make_async_copy(wout_hbm, wout, w_sem.at[1])
    load_qkv.start()
    load_out.start()

    x = x_ref[...].astype(F32)
    mean_here = jnp.sum(x, axis=1, keepdims=True) / width
    dev = x - mean_here
    m2_here = jnp.sum(dev * dev, axis=1, keepdims=True)
    stat_send[0, 0] = jnp.broadcast_to(mean_here, (rows, HS))
    stat_send[0, 1] = jnp.broadcast_to(m2_here, (rows, HS))
    gbuf[pl.ds(pl.multiple_of(col * rows, rows), rows), :] = g_ref[...]
    pl.semaphore_wait(barrier, peers)

    def remote(src, dst, ss, rs, device):
        return pltpu.make_async_remote_copy(
            src_ref=src, dst_ref=dst, send_sem=ss, recv_sem=rs, device_id=device, device_id_type=MESH
        )

    def slot(buf, chip, which):
        return buf.at[pl.ds(pl.multiple_of((chip * 2 + which) * rows, rows), rows), :]

    def z_copy(a, buf, b, up):
        here = slot(buf, b, core)
        ss = ag_up if up else ag_down
        return remote(here, here, ss.at[a, b], ag_recv.at[a, b], above if up else below)

    def s_copy(a, buf, b):
        here = slot(buf, b, core)
        return remote(here, here, sib_ss.at[a, b], sib_rs.at[a, b], sibling)

    def gather_step(a, buf, d):
        if d == 0:
            @pl.when(z < chips - 1)
            def _():
                z_copy(a, buf, z, True).start()

            @pl.when(z > 0)
            def _():
                z_copy(a, buf, z, False).start()

            s_copy(a, buf, z).start()
            return

        @pl.when(z >= d)
        def _():
            z_copy(a, buf, z - d, True).wait_recv()

            @pl.when(z < chips - 1)
            def _():
                z_copy(a, buf, z - d, True).start()

            s_copy(a, buf, z - d).start()

        @pl.when(z + d <= chips - 1)
        def _():
            z_copy(a, buf, z + d, False).wait_recv()

            @pl.when(z > 0)
            def _():
                z_copy(a, buf, z + d, False).start()

            s_copy(a, buf, z + d).start()

    def gather_end(a, buf):
        for b in range(chips):
            there = slot(buf, b, 1 - core)
            remote(there, there, sib_ss.at[a, b], sib_rs.at[a, b], sibling).wait_recv()

    def gather_drain(a, buf):
        for b in range(chips):
            s_copy(a, buf, b).wait_send()

            @pl.when((b <= z) & (z < chips - 1))
            def _():
                z_copy(a, buf, b, True).wait_send()

            @pl.when((b >= z) & (z > 0))
            def _():
                z_copy(a, buf, b, False).wait_send()

    gather_step(1, gbuf, 0)

    stats = remote(stat_send.at[0], stat_recv.at[0], stat_ss.at[0], stat_rs.at[0], across)
    stats.start()
    stats.wait_recv()
    mean_there = stat_recv[0, 0][:, :1]
    m2_there = stat_recv[0, 1][:, :1]
    gap = mean_here - mean_there
    average = (mean_here + mean_there) * 0.5
    variance = (m2_here + m2_there + gap * gap * (0.5 * width)) / (2.0 * width)
    rstd = lax.rsqrt(variance + EPS)
    rstd_buf[...] = jnp.broadcast_to(rstd, (rows, HS))
    hat = (x_ref[...].astype(F32) - average) * rstd
    xhat[...] = hat
    nbuf[pl.ds(pl.multiple_of(col * rows, rows), rows), :] = (hat * gain_ref[...]).astype(BF16)

    for d in range(chips):
        gather_step(0, nbuf, d)
        if d == chips - 2:
            gather_step(1, gbuf, 1)
    gather_end(0, nbuf)
    save_n = pltpu.make_async_copy(nbuf, n_out, out_sem.at[0])
    save_n.start()

    load_qkv.wait()
    wide = 3 * HS

    def head_cols(r, i):
        return pl.ds(pl.multiple_of((r * own_heads + i) * wide, HS), wide)

    def q_copy(i):
        return remote(q_send.at[i], q_recv.at[i], q_ss.at[i], q_rs.at[i], across)

    deep = 1024

    def pieces(k):
        return pl.ds(pl.multiple_of(k * deep, deep), deep)

    def project(cols):
        total[...] = jnp.zeros_like(total)

        def step(k, carry):
            total[...] += mm(nbuf[:, pieces(k)], wqkv[pieces(k), cols])
            return carry

        lax.fori_loop(0, width // deep, step, 0)

    def project_there(i, carry):
        project(head_cols(1 - row, i))
        q_send[i] = total[...].astype(BF16)
        q_copy(i).start()
        return carry

    lax.fori_loop(0, own_heads, project_there, 0)
    for d in range(2, chips):
        gather_step(1, gbuf, d)
        if d == 2:
            def project_here(i, carry):
                project(head_cols(row, i))
                q_copy(i).wait_recv()
                qkv[i] = (total[...] + q_recv[i].astype(F32)).astype(BF16)
                return carry

            lax.fori_loop(0, own_heads, project_here, 0)

    allowed = lax.broadcasted_iota(jnp.int32, (tokens, tokens), 1) <= lax.broadcasted_iota(
        jnp.int32, (tokens, tokens), 0
    )

    def ctx_copy(i):
        here = ctx.at[row * own_heads + i]
        return remote(here, here, c_ss.at[i], c_rs.at[i], across)

    def forward(i, carry):
        q = qkv[i, :, 0:HS]
        k = qkv[i, :, HS:2 * HS]
        v = qkv[i, :, 2 * HS:3 * HS]
        s = jnp.where(allowed, mm(q, k, NT) * scale, -jnp.inf)
        e = jnp.exp(s - jnp.max(s, axis=1, keepdims=True))
        p = e / jnp.sum(e, axis=1, keepdims=True)
        probs[i] = p
        ctx[row * own_heads + i] = mm(p.astype(BF16), v).astype(BF16)
        ctx_copy(i).start()
        return carry

    lax.fori_loop(0, own_heads, forward, 0)
    gather_end(1, gbuf)
    save_g = pltpu.make_async_copy(gbuf, g_out, out_sem.at[1])
    save_g.start()

    load_out.wait()
    span = own_heads * HS

    def out_rows(r):
        return pl.ds(pl.multiple_of(r * span, HS), span)

    def context_part(r):
        total[...] = jnp.zeros_like(total)

        def step(k, carry):
            total[...] += mm(gbuf[:, pieces(k)], wout[out_rows(r), pieces(k)], NT)
            return carry

        lax.fori_loop(0, width // deep, step, 0)

    context_part(1 - row)
    dc_send[...] = total[...].astype(BF16)
    dc_copy = remote(dc_send, dc_recv, dc_ss.at[0], dc_rs.at[0], across)
    dc_copy.start()
    context_part(row)
    dc_copy.wait_recv()
    dc = (total[...] + dc_recv[...].astype(F32)).astype(BF16)
    for i in range(own_heads):
        dctx[i] = dc[:, i * HS:(i + 1) * HS]

    def dq_copy(i):
        here = dqkv.at[:, head_cols(row, i)]
        return remote(here, here, dq_ss.at[i], dq_rs.at[i], across)

    def backward(i, carry):
        q = qkv[i, :, 0:HS]
        k = qkv[i, :, HS:2 * HS]
        v = qkv[i, :, 2 * HS:3 * HS]
        p = probs[i]
        dch = dctx[i]
        d_p = mm(dch, v, NT)
        delta = jnp.sum(p * d_p, axis=1, keepdims=True)
        d_s = (p * (d_p - delta) * scale).astype(BF16)
        d_q = mm(d_s, k)
        d_k = mm(d_s, q, TN)
        d_v = mm(p.astype(BF16), dch, TN)
        dqkv[:, head_cols(row, i)] = jnp.concatenate([d_q, d_k, d_v], axis=1).astype(BF16)
        dq_copy(i).start()
        return carry

    lax.fori_loop(0, own_heads, backward, 0)
    for i in range(own_heads):
        there = dqkv.at[:, head_cols(1 - row, i)]
        remote(there, there, dq_ss.at[i], dq_rs.at[i], across).wait_recv()
        other = ctx.at[(1 - row) * own_heads + i]
        remote(other, other, c_ss.at[i], c_rs.at[i], across).wait_recv()
    save_dqkv = pltpu.make_async_copy(dqkv, dqkv_out, out_sem.at[2])
    save_dqkv.start()
    save_ctx = pltpu.make_async_copy(ctx, ctx_out, out_sem.at[3])
    save_ctx.start()

    tile = 256

    def block_rows(b, which):
        return dqkv[pl.ds(pl.multiple_of((b * 2 + which) * rows, rows), rows), :]

    def partial_sums(b0, b1):
        left = jnp.concatenate(
            [block_rows(b0, core), block_rows(b1, core), block_rows(b0, 1 - core), block_rows(b1, 1 - core)],
            axis=0,
        )

        def step(t, carry):
            cols = pl.ds(pl.multiple_of(t * tile, tile), tile)
            out = mm(left, wqkv[cols, :], NT)
            acc[b0, :, cols] = out[0:rows]
            acc[b1, :, cols] = out[rows:2 * rows]
            sib_send[b0, :, cols] = out[2 * rows:3 * rows].astype(BF16)
            sib_send[b1, :, cols] = out[3 * rows:].astype(BF16)
            return carry

        lax.fori_loop(0, width // tile, step, 0)
        for b in (b0, b1):
            pair_copy(b).start()

    def pair_copy(b):
        return remote(sib_send.at[b], sib_recv.at[b], ps_ss.at[b], ps_rs.at[b], sibling)

    def line_copy(b, up):
        w = 0 if up else 1
        return remote(
            z_send.at[b], z_recv.at[w, b], rs_ss.at[b], rs_rs.at[w, b], above if up else below
        )

    def hop(d):
        @pl.when(z + d <= chips - 1)
        def _():
            b = z + d
            z_send[b] = acc[b].astype(BF16)

            @pl.when(z > 0)
            def _():
                line_copy(b, True).wait_recv()
                z_send[b] = (acc[b] + z_recv[0, b].astype(F32)).astype(BF16)

            line_copy(b, True).start()

        @pl.when(z - d >= 0)
        def _():
            b = z - d
            z_send[b] = acc[b].astype(BF16)

            @pl.when(z < chips - 1)
            def _():
                line_copy(b, False).wait_recv()
                z_send[b] = (acc[b] + z_recv[1, b].astype(F32)).astype(BF16)

            line_copy(b, False).start()

    def add_pair(b):
        pair_copy(b).wait_recv()
        acc[b] = acc[b] + sib_recv[b].astype(F32)

    far = chips - 1
    partial_sums(0, far)
    add_pair(0)
    add_pair(far)
    hop(far)
    partial_sums(1, 2)
    add_pair(1)
    add_pair(2)
    for d in range(far - 1, 0, -1):
        hop(d)

    @pl.when(z > 0)
    def _():
        line_copy(z, True).wait_recv()
        acc[z] = acc[z] + z_recv[0, z].astype(F32)

    @pl.when(z < chips - 1)
    def _():
        line_copy(z, False).wait_recv()
        acc[z] = acc[z] + z_recv[1, z].astype(F32)

    dn = acc[z]
    hat = xhat[...]
    gg = jnp.sum(dn * hat, axis=0, keepdims=True)
    gg_send[...] = gg

    def gg_copy(k):
        return remote(
            gg_send, gg_recv.at[col], gg_ss.at[k], gg_rs.at[col], (row, (col + k) % peers, dp)
        )

    for k in range(1, peers):
        gg_copy(k).start()
    sg = dn * gain_ref[...]
    first = jnp.sum(sg, axis=1, keepdims=True)
    second = jnp.sum(sg * hat, axis=1, keepdims=True)
    stat_send[1, 0] = jnp.broadcast_to(first, (rows, HS))
    stat_send[1, 1] = jnp.broadcast_to(second, (rows, HS))
    stats2 = remote(stat_send.at[1], stat_recv.at[1], stat_ss.at[1], stat_rs.at[1], across)
    stats2.start()
    stats2.wait_recv()
    first = (first + stat_recv[1, 0][:, :1]) / (2.0 * width)
    second = (second + stat_recv[1, 1][:, :1]) / (2.0 * width)
    sg = acc[z] * gain_ref[...]
    dx_ref[...] = (rstd_buf[:, :1] * (sg - first - xhat[...] * second)).astype(BF16)
    gg_recv[col] = gg_send[...]
    whole = jnp.zeros_like(gg)
    for k in range(1, peers):
        src = (col + k) % peers
        remote(gg_send, gg_recv.at[src], gg_ss.at[k], gg_rs.at[src], (row, src, dp)).wait_recv()
    for k in range(peers):
        whole = whole + gg_recv[k]
    dgain_ref[...] = whole

    stats.wait_send()
    stats2.wait_send()
    gather_drain(0, nbuf)
    gather_drain(1, gbuf)
    for i in range(own_heads):
        q_copy(i).wait_send()
        ctx_copy(i).wait_send()
        dq_copy(i).wait_send()
    dc_copy.wait_send()
    for b in range(chips):
        pair_copy(b).wait_send()

        @pl.when(b > z)
        def _():
            line_copy(b, True).wait_send()

        @pl.when(b < z)
        def _():
            line_copy(b, False).wait_send()

    for k in range(1, peers):
        gg_copy(k).wait_send()
    save_n.wait()
    save_g.wait()
    save_dqkv.wait()
    save_ctx.wait()


def pair_shards(layer_input, layer_norm_gain, w_qkv, w_out, out_grad):
    rows, width = layer_input.shape
    peers = lax.axis_size("col")
    chips = peers // 2
    tokens = rows * peers
    columns = w_qkv.shape[1]
    heads = columns // (3 * HS)
    own = heads // 2
    vmem = pl.BlockSpec(memory_space=pltpu.VMEM)
    hbm = pl.BlockSpec(memory_space=pl.ANY)
    dma = pltpu.SemaphoreType.DMA
    shape = jax.ShapeDtypeStruct
    dx, dgain, normed, grad, ctx, dqkv = pl.pallas_call(
        functools.partial(block_kernel, chips),
        out_shape=[
            shape((rows, width), BF16),
            shape((1, width), F32),
            shape((tokens, width), BF16),
            shape((tokens, width), BF16),
            shape((heads, tokens, HS), BF16),
            shape((tokens, columns), BF16),
        ],
        in_specs=[vmem, vmem, vmem, hbm, hbm],
        out_specs=[vmem, vmem, hbm, hbm, hbm, hbm],
        scratch_shapes=[
            pltpu.VMEM(w_qkv.shape, BF16),
            pltpu.VMEM(w_out.shape, BF16),
            pltpu.VMEM((tokens, width), BF16),
            pltpu.VMEM((tokens, width), BF16),
            pltpu.VMEM((rows, width), F32),
            pltpu.VMEM((rows, HS), F32),
            pltpu.VMEM((2, 2, rows, HS), F32),
            pltpu.VMEM((2, 2, rows, HS), F32),
            pltpu.VMEM((own, tokens, 3 * HS), BF16),
            pltpu.VMEM((own, tokens, 3 * HS), BF16),
            pltpu.VMEM((own, tokens, 3 * HS), BF16),
            pltpu.VMEM((own, tokens, tokens), F32),
            pltpu.VMEM((heads, tokens, HS), BF16),
            pltpu.VMEM((tokens, own * HS), BF16),
            pltpu.VMEM((tokens, own * HS), BF16),
            pltpu.VMEM((own, tokens, HS), BF16),
            pltpu.VMEM((tokens, columns), BF16),
            pltpu.VMEM((chips, rows, width), F32),
            pltpu.VMEM((chips, rows, width), BF16),
            pltpu.VMEM((chips, rows, width), BF16),
            pltpu.VMEM((chips, rows, width), BF16),
            pltpu.VMEM((2, chips, rows, width), BF16),
            pltpu.VMEM((1, width), F32),
            pltpu.VMEM((peers, 1, width), F32),
            pltpu.VMEM((tokens, 3 * HS), F32),
            dma((2,)), dma((4,)), dma((2,)), dma((2,)),
            dma((2, chips)), dma((2, chips)), dma((2, chips)), dma((2, chips)), dma((2, chips)),
            dma((own,)), dma((own,)), dma((own,)), dma((own,)),
            dma((1,)), dma((1,)), dma((own,)), dma((own,)),
            dma((chips,)), dma((chips,)), dma((chips,)), dma((2, chips)),
            dma((peers,)), dma((peers,)),
        ],
        compiler_params=pltpu.CompilerParams(
            collective_id=0, has_side_effects=True, vmem_limit_bytes=63 * 2**20
        ),
    )(layer_input, layer_norm_gain.reshape(1, width), out_grad, w_qkv, w_out)
    grad_wqkv = mm(normed, dqkv, TN).astype(BF16)
    context = ctx.transpose(1, 0, 2).reshape(tokens, heads * HS)
    grad_wout = mm(context, grad, TN).astype(BF16)
    return dx, dgain.reshape(width), grad_wqkv, grad_wout


def choose(layer_input, layer_norm_gain, w_qkv, w_out, out_grad):
    paired = lax.axis_size("row") == 2 and lax.axis_size("col") == 8
    sized = layer_input.shape[1] % 1024 == 0 and layer_input.shape[0] == 32
    body = pair_shards if paired and sized and w_qkv.shape[1] == 18 * HS else shards
    return body(layer_input, layer_norm_gain, w_qkv, w_out, out_grad)


def solution(mesh):
    in_specs = (
        P(("dp", "col"), "row"),
        P("row"),
        P("row", "col"),
        P("col", "row"),
        P(("dp", "col"), "row"),
    )
    out_specs = (
        P(("dp", "col"), "row"),
        P(("dp", "row")),
        P(("dp", "row"), "col"),
        P(("dp", "col"), "row"),
    )
    return jax.shard_map(choose, mesh=mesh, in_specs=in_specs, out_specs=out_specs, check_vma=False)
```

```python
import functools
import math

import jax
import jax.numpy as jnp
from jax import lax
from jax.experimental import pallas as pl
from jax.experimental.pallas import tpu as pltpu
from jax.sharding import PartitionSpec as P

HS = 128


EPS = 1e-05


def shards(layer_input, layer_norm_gain, w_qkv, w_out, out_grad):
    rows_here, features_here = layer_input.shape
    col_count = lax.axis_size("col")
    row_count = lax.axis_size("row")
    tokens = rows_here * col_count
    tok_row = tokens // row_count
    feature_width = features_here * row_count
    heads_here = w_qkv.shape[1] // (3 * HS)
    scale = 1.0 / math.sqrt(HS)
    input_float = layer_input.astype(jnp.float32)
    average = lax.psum(jnp.sum(input_float, axis=1), "row") / feature_width
    centered_input = input_float - average[:, None]
    variance = lax.psum(jnp.sum(centered_input * centered_input, axis=1), "row") / feature_width
    inverse_deviation = lax.rsqrt(variance + EPS)
    standardized_input = centered_input * inverse_deviation[:, None]
    normalized_output = (standardized_input * layer_norm_gain[None, :]).astype(jnp.bfloat16)
    normed_all = lax.all_gather(normalized_output, "col", axis=0, tiled=True)
    first_query = lax.axis_index("row") * tok_row
    piece = normed_all
    owned = lax.psum_scatter(
        jnp.dot(piece, w_qkv, preferred_element_type=jnp.float32),
        "row",
        scatter_dimension=0,
        tiled=True,
    ).astype(jnp.bfloat16)
    owned = owned.reshape(tok_row, heads_here, 3, HS)
    query = owned[:, :, 0]
    key_value = lax.all_gather(owned[:, :, 1:], "row", axis=0, tiled=True)
    keys = key_value[:, :, 0]
    values = key_value[:, :, 1]
    query_pos = first_query + jnp.arange(tok_row)
    key_pos = jnp.arange(tokens)
    allowed = key_pos[None, :] <= query_pos[:, None]
    scores = jnp.einsum("qhe,khe->hqk", query, keys, preferred_element_type=jnp.float32) * scale
    scores = jnp.where(allowed[None], scores, -jnp.inf)
    highest = jnp.max(scores, axis=2, keepdims=True)
    powers = jnp.exp(scores - highest)
    totals = jnp.sum(powers, axis=2, keepdims=True)
    probs = powers / totals
    probs_b = probs.astype(jnp.bfloat16)
    context = jnp.einsum(
        "hqk,khe->qhe", probs_b, values, preferred_element_type=jnp.float32
    ).astype(jnp.bfloat16)
    context_all = lax.all_gather(
        context.reshape(tok_row, heads_here * HS), "row", axis=0, tiled=True
    )
    grad_all = lax.all_gather(out_grad, "col", axis=0, tiled=True)
    grad_wout = lax.dot_general(
        context_all, grad_all, (((0,), (0,)), ((), ())), preferred_element_type=jnp.float32
    ).astype(jnp.bfloat16)
    piece = grad_all
    d_context = lax.psum_scatter(
        lax.dot_general(piece, w_out, (((1,), (1,)), ((), ())), preferred_element_type=jnp.float32),
        "row",
        scatter_dimension=0,
        tiled=True,
    ).astype(jnp.bfloat16)
    d_context = d_context.reshape(tok_row, heads_here, HS)
    d_probs = jnp.einsum("qhe,khe->hqk", d_context, values, preferred_element_type=jnp.float32)
    delta = jnp.sum(probs * d_probs, axis=2, keepdims=True)
    d_scores = (probs * (d_probs - delta) * scale).astype(jnp.bfloat16)
    d_query = jnp.einsum("hqk,khe->qhe", d_scores, keys, preferred_element_type=jnp.float32).astype(
        jnp.bfloat16
    )
    d_keys = jnp.einsum("hqk,qhe->khe", d_scores, query, preferred_element_type=jnp.float32)
    d_values = jnp.einsum("hqk,qhe->khe", probs_b, d_context, preferred_element_type=jnp.float32)
    d_pairs = jnp.stack([d_keys, d_values], axis=2)
    pair_owned = lax.psum_scatter(d_pairs, "row", scatter_dimension=0, tiled=True).astype(
        jnp.bfloat16
    )
    owned_grad = jnp.concatenate([d_query[:, :, None], pair_owned], axis=2)
    owned_grad = owned_grad.reshape(tok_row, heads_here * 3 * HS)
    d_qkv_all = lax.all_gather(owned_grad, "row", axis=0, tiled=True)
    grad_wqkv = lax.dot_general(
        normed_all, d_qkv_all, (((0,), (0,)), ((), ())), preferred_element_type=jnp.float32
    ).astype(jnp.bfloat16)
    piece = d_qkv_all
    normalized_gradient = lax.psum_scatter(
        lax.dot_general(piece, w_qkv, (((1,), (1,)), ((), ())), preferred_element_type=jnp.float32),
        "col",
        scatter_dimension=0,
        tiled=True,
    )
    gain_gradient = lax.psum(jnp.sum(normalized_gradient * standardized_input, axis=0), "col")
    scaled_gradient = normalized_gradient * layer_norm_gain[None, :]
    first_term_sum, second_term_sum = lax.psum(
        (jnp.sum(scaled_gradient, axis=1), jnp.sum(scaled_gradient * standardized_input, axis=1)),
        "row",
    )
    input_gradient = inverse_deviation[:, None] * (
        scaled_gradient
        - first_term_sum[:, None] / feature_width
        - standardized_input * (second_term_sum[:, None] / feature_width)
    )
    return (input_gradient.astype(jnp.bfloat16), gain_gradient, grad_wqkv, grad_wout)

MESH = pl.DeviceIdType.MESH
F32 = jnp.float32
BF16 = jnp.bfloat16
NT = (((1,), (1,)), ((), ()))
TN = (((0,), (0,)), ((), ()))
NN = (((1,), (0,)), ((), ()))


def mm(a, b, dims=NN):
    return lax.dot_general(a, b, dims, preferred_element_type=F32)


def block_kernel(
    chips, x_ref, gain_ref, g_ref, wqkv_hbm, wout_hbm,
    n_out, g_out, ctx_out, dqkv_out, xhat_out, rstd_out, here_out, up_out, down_out, pass_out,
    wqkv, wout, nbuf, gbuf, xhat, rstd_buf, stat_send, stat_recv,
    q_send, q_recv, qkv, probs, ctx, dc_send, dc_recv, dctx, dqkv,
    acc, sib_send, sib_recv, z_send, z_pass, z_recv, total,
    w_sem, out_sem, ctx_sem, stat_ss, stat_rs, ag_up, ag_down, ag_recv, sib_ss, sib_rs,
    q_ss, q_rs, c_ss, c_rs, dc_ss, dc_rs, dq_ss, dq_rs,
    ps_ss, ps_rs, rs_ss, rs_rs,
):
    row = lax.axis_index("row")
    col = lax.axis_index("col")
    dp = lax.axis_index("dp")
    z = col // 2
    core = col % 2
    rows, width = x_ref.shape
    tokens = nbuf.shape[0]
    own_heads = qkv.shape[0]
    scale = 1.0 / math.sqrt(HS)
    across = (1 - row, col, dp)
    sibling = (row, z * 2 + 1 - core, dp)
    above = (row, jnp.minimum(z + 1, chips - 1) * 2 + core, dp)
    below = (row, jnp.maximum(z - 1, 0) * 2 + core, dp)
    peers = 2 * chips

    barrier = pltpu.get_barrier_semaphore()
    pl.semaphore_signal(barrier, inc=1, device_id=across, device_id_type=MESH)
    for k in range(1, peers):
        pl.semaphore_signal(
            barrier, inc=1, device_id=(row, (col + k) % peers, dp), device_id_type=MESH
        )
    load_qkv = pltpu.make_async_copy(wqkv_hbm, wqkv, w_sem.at[0])
    load_out = pltpu.make_async_copy(wout_hbm, wout, w_sem.at[1])
    load_qkv.start()
    load_out.start()

    x = x_ref[...].astype(F32)
    mean_here = jnp.sum(x, axis=1, keepdims=True) / width
    dev = x - mean_here
    m2_here = jnp.sum(dev * dev, axis=1, keepdims=True)
    stat_send[0, 0] = jnp.broadcast_to(mean_here, (rows, HS))
    stat_send[0, 1] = jnp.broadcast_to(m2_here, (rows, HS))
    gbuf[pl.ds(pl.multiple_of(col * rows, rows), rows), :] = g_ref[...]
    pl.semaphore_wait(barrier, peers)

    def remote(src, dst, ss, rs, device):
        return pltpu.make_async_remote_copy(
            src_ref=src, dst_ref=dst, send_sem=ss, recv_sem=rs, device_id=device, device_id_type=MESH
        )

    def slot(buf, chip, which):
        return buf.at[pl.ds(pl.multiple_of((chip * 2 + which) * rows, rows), rows), :]

    def z_copy(a, buf, b, up):
        here = slot(buf, b, core)
        ss = ag_up if up else ag_down
        return remote(here, here, ss.at[a, b], ag_recv.at[a, b], above if up else below)

    def s_copy(a, buf, b):
        here = slot(buf, b, core)
        return remote(here, here, sib_ss.at[a, b], sib_rs.at[a, b], sibling)

    def gather_step(a, buf, d):
        if d == 0:
            @pl.when(z < chips - 1)
            def _():
                z_copy(a, buf, z, True).start()

            @pl.when(z > 0)
            def _():
                z_copy(a, buf, z, False).start()

            s_copy(a, buf, z).start()
            return

        @pl.when(z >= d)
        def _():
            z_copy(a, buf, z - d, True).wait_recv()

            @pl.when(z < chips - 1)
            def _():
                z_copy(a, buf, z - d, True).start()

            s_copy(a, buf, z - d).start()

        @pl.when(z + d <= chips - 1)
        def _():
            z_copy(a, buf, z + d, False).wait_recv()

            @pl.when(z > 0)
            def _():
                z_copy(a, buf, z + d, False).start()

            s_copy(a, buf, z + d).start()

    def gather_end(a, buf):
        for b in range(chips):
            there = slot(buf, b, 1 - core)
            remote(there, there, sib_ss.at[a, b], sib_rs.at[a, b], sibling).wait_recv()

    def gather_drain(a, buf):
        for b in range(chips):
            s_copy(a, buf, b).wait_send()

            @pl.when((b <= z) & (z < chips - 1))
            def _():
                z_copy(a, buf, b, True).wait_send()

            @pl.when((b >= z) & (z > 0))
            def _():
                z_copy(a, buf, b, False).wait_send()

    gather_step(1, gbuf, 0)

    stats = remote(stat_send.at[0], stat_recv.at[0], stat_ss.at[0], stat_rs.at[0], across)
    stats.start()
    stats.wait_recv()
    mean_there = stat_recv[0, 0][:, :1]
    m2_there = stat_recv[0, 1][:, :1]
    gap = mean_here - mean_there
    average = (mean_here + mean_there) * 0.5
    variance = (m2_here + m2_there + gap * gap * (0.5 * width)) / (2.0 * width)
    rstd = lax.rsqrt(variance + EPS)
    rstd_buf[...] = jnp.broadcast_to(rstd, (rows, HS))
    hat = (x_ref[...].astype(F32) - average) * rstd
    xhat[...] = hat
    nbuf[pl.ds(pl.multiple_of(col * rows, rows), rows), :] = (hat * gain_ref[...]).astype(BF16)

    for d in range(chips):
        gather_step(0, nbuf, d)
        if d == chips - 2:
            gather_step(1, gbuf, 1)
    gather_end(0, nbuf)
    save_n = pltpu.make_async_copy(nbuf, n_out, out_sem.at[0])
    save_n.start()

    load_qkv.wait()
    wide = 3 * HS

    def head_cols(r, i):
        return pl.ds(pl.multiple_of((r * own_heads + i) * wide, HS), wide)

    def q_copy(i):
        return remote(q_send.at[i], q_recv.at[i], q_ss.at[i], q_rs.at[i], across)

    deep = 1024

    def pieces(k):
        return pl.ds(pl.multiple_of(k * deep, deep), deep)

    def project(cols):
        total[...] = jnp.zeros_like(total)

        def step(k, carry):
            total[...] += mm(nbuf[:, pieces(k)], wqkv[pieces(k), cols])
            return carry

        lax.fori_loop(0, width // deep, step, 0)

    def project_there(i, carry):
        project(head_cols(1 - row, i))
        q_send[i] = total[...].astype(BF16)
        q_copy(i).start()
        return carry

    lax.fori_loop(0, own_heads, project_there, 0)
    for d in range(2, chips):
        gather_step(1, gbuf, d)
        if d == 2:
            def project_here(i, carry):
                project(head_cols(row, i))
                q_copy(i).wait_recv()
                qkv[i] = (total[...] + q_recv[i].astype(F32)).astype(BF16)
                return carry

            lax.fori_loop(0, own_heads, project_here, 0)

    allowed = lax.broadcasted_iota(jnp.int32, (tokens, tokens), 1) <= lax.broadcasted_iota(
        jnp.int32, (tokens, tokens), 0
    )

    def ctx_copy(i):
        here = ctx.at[row * own_heads + i]
        return remote(here, here, c_ss.at[i], c_rs.at[i], across)

    def forward(i, carry):
        q = qkv[i, :, 0:HS]
        k = qkv[i, :, HS:2 * HS]
        v = qkv[i, :, 2 * HS:3 * HS]
        s = jnp.where(allowed, mm(q, k, NT) * scale, -jnp.inf)
        e = jnp.exp(s - jnp.max(s, axis=1, keepdims=True))
        p = e / jnp.sum(e, axis=1, keepdims=True)
        probs[i] = p
        ctx[row * own_heads + i] = mm(p.astype(BF16), v).astype(BF16)
        ctx_copy(i).start()
        return carry

    lax.fori_loop(0, own_heads, forward, 0)
    gather_end(1, gbuf)
    save_g = pltpu.make_async_copy(gbuf, g_out, out_sem.at[1])
    save_g.start()

    load_out.wait()
    span = own_heads * HS

    def out_rows(r):
        return pl.ds(pl.multiple_of(r * span, HS), span)

    def context_part(r):
        total[...] = jnp.zeros_like(total)

        def step(k, carry):
            total[...] += mm(gbuf[:, pieces(k)], wout[out_rows(r), pieces(k)], NT)
            return carry

        lax.fori_loop(0, width // deep, step, 0)

    context_part(1 - row)
    dc_send[...] = total[...].astype(BF16)
    dc_copy = remote(dc_send, dc_recv, dc_ss.at[0], dc_rs.at[0], across)
    dc_copy.start()
    context_part(row)
    dc_copy.wait_recv()
    dc = (total[...] + dc_recv[...].astype(F32)).astype(BF16)
    for i in range(own_heads):
        dctx[i] = dc[:, i * HS:(i + 1) * HS]

    def dq_copy(i):
        here = dqkv.at[:, head_cols(row, i)]
        return remote(here, here, dq_ss.at[i], dq_rs.at[i], across)

    def backward(i, carry):
        q = qkv[i, :, 0:HS]
        k = qkv[i, :, HS:2 * HS]
        v = qkv[i, :, 2 * HS:3 * HS]
        p = probs[i]
        dch = dctx[i]
        d_p = mm(dch, v, NT)
        delta = jnp.sum(p * d_p, axis=1, keepdims=True)
        d_s = (p * (d_p - delta) * scale).astype(BF16)
        d_q = mm(d_s, k)
        d_k = mm(d_s, q, TN)
        d_v = mm(p.astype(BF16), dch, TN)
        dqkv[:, head_cols(row, i)] = jnp.concatenate([d_q, d_k, d_v], axis=1).astype(BF16)
        dq_copy(i).start()
        return carry

    lax.fori_loop(0, own_heads, backward, 0)
    for i in range(own_heads):
        there = dqkv.at[:, head_cols(1 - row, i)]
        remote(there, there, dq_ss.at[i], dq_rs.at[i], across).wait_recv()
        other = ctx.at[(1 - row) * own_heads + i]
        remote(other, other, c_ss.at[i], c_rs.at[i], across).wait_recv()
    save_dqkv = pltpu.make_async_copy(dqkv, dqkv_out, out_sem.at[2])
    save_dqkv.start()
    ctx_saves = []
    for h in range(2 * own_heads):
        to = ctx_out.at[:, h * HS:(h + 1) * HS]
        ctx_saves.append(pltpu.make_async_copy(ctx.at[h], to, ctx_sem.at[h]))
        ctx_saves[h].start()

    tile = 256

    def block_rows(b, which):
        return dqkv[pl.ds(pl.multiple_of((b * 2 + which) * rows, rows), rows), :]

    def partial_sums(b0, b1):
        left = jnp.concatenate(
            [block_rows(b0, core), block_rows(b1, core), block_rows(b0, 1 - core), block_rows(b1, 1 - core)],
            axis=0,
        )

        def step(t, carry):
            cols = pl.ds(pl.multiple_of(t * tile, tile), tile)
            out = mm(left, wqkv[cols, :], NT)
            acc[b0, :, cols] = out[0:rows]
            acc[b1, :, cols] = out[rows:2 * rows]
            sib_send[b0, :, cols] = out[2 * rows:3 * rows].astype(BF16)
            sib_send[b1, :, cols] = out[3 * rows:].astype(BF16)
            return carry

        lax.fori_loop(0, width // tile, step, 0)
        for b in (b0, b1):
            pair_copy(b).start()

    def pair_copy(b):
        return remote(sib_send.at[b], sib_recv.at[b], ps_ss.at[b], ps_rs.at[b], sibling)

    def line_copy(b, up):
        w = 0 if up else 1
        return remote(z_send, z_recv.at[w], rs_ss.at[w], rs_rs.at[w], above if up else below)

    def hop_far():
        @pl.when(z == 0)
        def _():
            z_send[...] = acc[far].astype(BF16)
            line_copy(far, True).start()

        @pl.when(z == far)
        def _():
            z_send[...] = acc[0].astype(BF16)
            line_copy(0, False).start()

    def add_pair(b):
        pair_copy(b).wait_recv()
        acc[b] = acc[b] + sib_recv[b].astype(F32)

    far = chips - 1
    partial_sums(0, far)
    add_pair(0)
    add_pair(far)
    hop_far()
    partial_sums(1, 2)
    add_pair(1)
    add_pair(2)

    half = chips // 2
    b_pass = jnp.where(z < half, z + half, z - half)
    z_pass[...] = acc[b_pass].astype(BF16)

    @pl.when(z == 1)
    def _():
        line_copy(far, True).wait_recv()
        z_pass[...] = (acc[far] + z_recv[0].astype(F32)).astype(BF16)

    @pl.when(z == far - 1)
    def _():
        line_copy(0, False).wait_recv()
        z_pass[...] = (acc[0] + z_recv[1].astype(F32)).astype(BF16)

    saves = [
        pltpu.make_async_copy(xhat, xhat_out, out_sem.at[4]),
        pltpu.make_async_copy(rstd_buf, rstd_out, out_sem.at[5]),
        pltpu.make_async_copy(acc.at[z], here_out, out_sem.at[6]),
        pltpu.make_async_copy(acc.at[jnp.minimum(z + 1, far)], up_out, out_sem.at[7]),
        pltpu.make_async_copy(acc.at[jnp.maximum(z - 1, 0)], down_out, out_sem.at[8]),
        pltpu.make_async_copy(z_pass, pass_out, out_sem.at[9]),
    ]
    for save in saves:
        save.start()

    stats.wait_send()
    gather_drain(0, nbuf)
    gather_drain(1, gbuf)
    for i in range(own_heads):
        q_copy(i).wait_send()
        ctx_copy(i).wait_send()
        dq_copy(i).wait_send()
    dc_copy.wait_send()
    for b in range(chips):
        pair_copy(b).wait_send()

    @pl.when(z == 0)
    def _():
        line_copy(far, True).wait_send()

    @pl.when(z == far)
    def _():
        line_copy(0, False).wait_send()

    save_n.wait()
    save_g.wait()
    save_dqkv.wait()
    for save in saves:
        save.wait()
    for save in ctx_saves:
        save.wait()


def norm_kernel(
    here_ref, from_below, from_above, xhat_ref, rstd_ref, gain_ref, dx_ref, dgain_ref,
    dn_buf, stat_send, stat_recv, gg_send, gg_recv, stat_ss, stat_rs, gg_ss, gg_rs,
):
    row = lax.axis_index("row")
    col = lax.axis_index("col")
    dp = lax.axis_index("dp")
    rows, width = here_ref.shape
    peers = gg_recv.shape[0]
    across = (1 - row, col, dp)

    barrier = pltpu.get_barrier_semaphore()
    pl.semaphore_signal(barrier, inc=1, device_id=across, device_id_type=MESH)
    for k in range(1, peers):
        pl.semaphore_signal(
            barrier, inc=1, device_id=(row, (col + k) % peers, dp), device_id_type=MESH
        )
    dn = here_ref[...] + from_below[...].astype(F32) + from_above[...].astype(F32)
    sg = dn * gain_ref[...]
    dn_buf[...] = sg
    hat = xhat_ref[...]
    first = jnp.sum(sg, axis=1, keepdims=True)
    second = jnp.sum(sg * hat, axis=1, keepdims=True)
    stat_send[0] = jnp.broadcast_to(first, (rows, HS))
    stat_send[1] = jnp.broadcast_to(second, (rows, HS))
    gg_send[...] = jnp.sum(dn * hat, axis=0, keepdims=True)
    pl.semaphore_wait(barrier, peers)

    stats = pltpu.make_async_remote_copy(
        src_ref=stat_send, dst_ref=stat_recv, send_sem=stat_ss.at[0], recv_sem=stat_rs.at[0],
        device_id=across, device_id_type=MESH,
    )
    stats.start()

    def gg_copy(k, source):
        return pltpu.make_async_remote_copy(
            src_ref=gg_send, dst_ref=gg_recv.at[source], send_sem=gg_ss.at[k], recv_sem=gg_rs.at[source],
            device_id=(row, (col + k) % peers, dp), device_id_type=MESH,
        )

    for k in range(1, peers):
        gg_copy(k, col).start()
    stats.wait_recv()
    first = (first + stat_recv[0][:, :1]) / (2.0 * width)
    second = (second + stat_recv[1][:, :1]) / (2.0 * width)
    dx_ref[...] = (rstd_ref[:, :1] * (dn_buf[...] - first - xhat_ref[...] * second)).astype(BF16)
    gg_recv[col] = gg_send[...]
    for k in range(1, peers):
        gg_copy(k, (col + k) % peers).wait_recv()
    whole = gg_recv[0]
    for k in range(1, peers):
        whole = whole + gg_recv[k]
    dgain_ref[...] = whole
    stats.wait_send()
    for k in range(1, peers):
        gg_copy(k, col).wait_send()


def pair_shards(layer_input, layer_norm_gain, w_qkv, w_out, out_grad):
    rows, width = layer_input.shape
    peers = lax.axis_size("col")
    chips = peers // 2
    tokens = rows * peers
    columns = w_qkv.shape[1]
    heads = columns // (3 * HS)
    own = heads // 2
    vmem = pl.BlockSpec(memory_space=pltpu.VMEM)
    hbm = pl.BlockSpec(memory_space=pl.ANY)
    dma = pltpu.SemaphoreType.DMA
    shape = jax.ShapeDtypeStruct
    normed, grad, context, dqkv, xhat, rstd, here, up, down, onward = pl.pallas_call(
        functools.partial(block_kernel, chips),
        out_shape=[
            shape((tokens, width), BF16),
            shape((tokens, width), BF16),
            shape((tokens, heads * HS), BF16),
            shape((tokens, columns), BF16),
            shape((rows, width), F32),
            shape((rows, HS), F32),
            shape((rows, width), F32),
            shape((rows, width), F32),
            shape((rows, width), F32),
            shape((rows, width), BF16),
        ],
        in_specs=[vmem, vmem, vmem, hbm, hbm],
        out_specs=[hbm] * 10,
        scratch_shapes=[
            pltpu.VMEM(w_qkv.shape, BF16),
            pltpu.VMEM(w_out.shape, BF16),
            pltpu.VMEM((tokens, width), BF16),
            pltpu.VMEM((tokens, width), BF16),
            pltpu.VMEM((rows, width), F32),
            pltpu.VMEM((rows, HS), F32),
            pltpu.VMEM((1, 2, rows, HS), F32),
            pltpu.VMEM((1, 2, rows, HS), F32),
            pltpu.VMEM((own, tokens, 3 * HS), BF16),
            pltpu.VMEM((own, tokens, 3 * HS), BF16),
            pltpu.VMEM((own, tokens, 3 * HS), BF16),
            pltpu.VMEM((own, tokens, tokens), F32),
            pltpu.VMEM((heads, tokens, HS), BF16),
            pltpu.VMEM((tokens, own * HS), BF16),
            pltpu.VMEM((tokens, own * HS), BF16),
            pltpu.VMEM((own, tokens, HS), BF16),
            pltpu.VMEM((tokens, columns), BF16),
            pltpu.VMEM((chips, rows, width), F32),
            pltpu.VMEM((chips, rows, width), BF16),
            pltpu.VMEM((chips, rows, width), BF16),
            pltpu.VMEM((rows, width), BF16),
            pltpu.VMEM((rows, width), BF16),
            pltpu.VMEM((2, rows, width), BF16),
            pltpu.VMEM((tokens, 3 * HS), F32),
            dma((2,)), dma((10,)), dma((heads,)), dma((1,)), dma((1,)),
            dma((2, chips)), dma((2, chips)), dma((2, chips)), dma((2, chips)), dma((2, chips)),
            dma((own,)), dma((own,)), dma((own,)), dma((own,)),
            dma((1,)), dma((1,)), dma((own,)), dma((own,)),
            dma((chips,)), dma((chips,)), dma((2,)), dma((2,)),
        ],
        compiler_params=pltpu.CompilerParams(
            collective_id=0, has_side_effects=True, vmem_limit_bytes=63 * 2**20
        ),
    )(layer_input, layer_norm_gain.reshape(1, width), out_grad, w_qkv, w_out)
    half = chips // 2
    both = range(2)
    rise = [(2 * z + c, 2 * z + 2 + c) for z in range(chips - 1) for c in both]
    fall = [(b, a) for a, b in rise]
    rise_first = [(2 * z + c, 2 * z + 2 + c) for z in range(half) for c in both]
    fall_first = [(2 * z + c, 2 * z - 2 + c) for z in range(half, chips) for c in both]
    got_up = lax.ppermute(onward, "col", rise_first)
    got_down = lax.ppermute(onward, "col", fall_first)
    grad_wqkv = mm(normed, dqkv, TN).astype(BF16)
    next_up = (up + got_up.astype(F32)).astype(BF16)
    next_down = (down + got_down.astype(F32)).astype(BF16)
    from_below = lax.ppermute(next_up, "col", rise)
    from_above = lax.ppermute(next_down, "col", fall)
    grad_wout = mm(context, grad, TN).astype(BF16)
    dx, dgain = pl.pallas_call(
        norm_kernel,
        out_shape=[shape((rows, width), BF16), shape((1, width), F32)],
        in_specs=[vmem] * 6,
        out_specs=[vmem] * 2,
        scratch_shapes=[
            pltpu.VMEM((rows, width), F32),
            pltpu.VMEM((2, rows, HS), F32),
            pltpu.VMEM((2, rows, HS), F32),
            pltpu.VMEM((1, width), F32),
            pltpu.VMEM((peers, 1, width), F32),
            dma((1,)), dma((1,)), dma((peers,)), dma((peers,)),
        ],
        compiler_params=pltpu.CompilerParams(
            collective_id=1, has_side_effects=True, vmem_limit_bytes=24 * 2**20
        ),
    )(here, from_below, from_above, xhat, rstd, layer_norm_gain.reshape(1, width))
    return dx, dgain.reshape(width), grad_wqkv, grad_wout


def choose(layer_input, layer_norm_gain, w_qkv, w_out, out_grad):
    paired = lax.axis_size("row") == 2 and lax.axis_size("col") == 8
    sized = layer_input.shape[1] % 1024 == 0 and layer_input.shape[0] == 32
    body = pair_shards if paired and sized and w_qkv.shape[1] == 18 * HS else shards
    return body(layer_input, layer_norm_gain, w_qkv, w_out, out_grad)


def solution(mesh):
    in_specs = (
        P(("dp", "col"), "row"),
        P("row"),
        P("row", "col"),
        P("col", "row"),
        P(("dp", "col"), "row"),
    )
    out_specs = (
        P(("dp", "col"), "row"),
        P(("dp", "row")),
        P(("dp", "row"), "col"),
        P(("dp", "col"), "row"),
    )
    return jax.shard_map(choose, mesh=mesh, in_specs=in_specs, out_specs=out_specs, check_vma=False)
```

```python
import functools
import math

import jax
import jax.numpy as jnp
from jax import lax
from jax.experimental import pallas as pl
from jax.experimental.pallas import tpu as pltpu
from jax.sharding import PartitionSpec as P

HS = 128


EPS = 1e-05


def shards(layer_input, layer_norm_gain, w_qkv, w_out, out_grad):
    rows_here, features_here = layer_input.shape
    col_count = lax.axis_size("col")
    row_count = lax.axis_size("row")
    tokens = rows_here * col_count
    tok_row = tokens // row_count
    feature_width = features_here * row_count
    heads_here = w_qkv.shape[1] // (3 * HS)
    scale = 1.0 / math.sqrt(HS)
    input_float = layer_input.astype(jnp.float32)
    average = lax.psum(jnp.sum(input_float, axis=1), "row") / feature_width
    centered_input = input_float - average[:, None]
    variance = lax.psum(jnp.sum(centered_input * centered_input, axis=1), "row") / feature_width
    inverse_deviation = lax.rsqrt(variance + EPS)
    standardized_input = centered_input * inverse_deviation[:, None]
    normalized_output = (standardized_input * layer_norm_gain[None, :]).astype(jnp.bfloat16)
    normed_all = lax.all_gather(normalized_output, "col", axis=0, tiled=True)
    first_query = lax.axis_index("row") * tok_row
    piece = normed_all
    owned = lax.psum_scatter(
        jnp.dot(piece, w_qkv, preferred_element_type=jnp.float32),
        "row",
        scatter_dimension=0,
        tiled=True,
    ).astype(jnp.bfloat16)
    owned = owned.reshape(tok_row, heads_here, 3, HS)
    query = owned[:, :, 0]
    key_value = lax.all_gather(owned[:, :, 1:], "row", axis=0, tiled=True)
    keys = key_value[:, :, 0]
    values = key_value[:, :, 1]
    query_pos = first_query + jnp.arange(tok_row)
    key_pos = jnp.arange(tokens)
    allowed = key_pos[None, :] <= query_pos[:, None]
    scores = jnp.einsum("qhe,khe->hqk", query, keys, preferred_element_type=jnp.float32) * scale
    scores = jnp.where(allowed[None], scores, -jnp.inf)
    highest = jnp.max(scores, axis=2, keepdims=True)
    powers = jnp.exp(scores - highest)
    totals = jnp.sum(powers, axis=2, keepdims=True)
    probs = powers / totals
    probs_b = probs.astype(jnp.bfloat16)
    context = jnp.einsum(
        "hqk,khe->qhe", probs_b, values, preferred_element_type=jnp.float32
    ).astype(jnp.bfloat16)
    context_all = lax.all_gather(
        context.reshape(tok_row, heads_here * HS), "row", axis=0, tiled=True
    )
    grad_all = lax.all_gather(out_grad, "col", axis=0, tiled=True)
    grad_wout = lax.dot_general(
        context_all, grad_all, (((0,), (0,)), ((), ())), preferred_element_type=jnp.float32
    ).astype(jnp.bfloat16)
    piece = grad_all
    d_context = lax.psum_scatter(
        lax.dot_general(piece, w_out, (((1,), (1,)), ((), ())), preferred_element_type=jnp.float32),
        "row",
        scatter_dimension=0,
        tiled=True,
    ).astype(jnp.bfloat16)
    d_context = d_context.reshape(tok_row, heads_here, HS)
    d_probs = jnp.einsum("qhe,khe->hqk", d_context, values, preferred_element_type=jnp.float32)
    delta = jnp.sum(probs * d_probs, axis=2, keepdims=True)
    d_scores = (probs * (d_probs - delta) * scale).astype(jnp.bfloat16)
    d_query = jnp.einsum("hqk,khe->qhe", d_scores, keys, preferred_element_type=jnp.float32).astype(
        jnp.bfloat16
    )
    d_keys = jnp.einsum("hqk,qhe->khe", d_scores, query, preferred_element_type=jnp.float32)
    d_values = jnp.einsum("hqk,qhe->khe", probs_b, d_context, preferred_element_type=jnp.float32)
    d_pairs = jnp.stack([d_keys, d_values], axis=2)
    pair_owned = lax.psum_scatter(d_pairs, "row", scatter_dimension=0, tiled=True).astype(
        jnp.bfloat16
    )
    owned_grad = jnp.concatenate([d_query[:, :, None], pair_owned], axis=2)
    owned_grad = owned_grad.reshape(tok_row, heads_here * 3 * HS)
    d_qkv_all = lax.all_gather(owned_grad, "row", axis=0, tiled=True)
    grad_wqkv = lax.dot_general(
        normed_all, d_qkv_all, (((0,), (0,)), ((), ())), preferred_element_type=jnp.float32
    ).astype(jnp.bfloat16)
    piece = d_qkv_all
    normalized_gradient = lax.psum_scatter(
        lax.dot_general(piece, w_qkv, (((1,), (1,)), ((), ())), preferred_element_type=jnp.float32),
        "col",
        scatter_dimension=0,
        tiled=True,
    )
    gain_gradient = lax.psum(jnp.sum(normalized_gradient * standardized_input, axis=0), "col")
    scaled_gradient = normalized_gradient * layer_norm_gain[None, :]
    first_term_sum, second_term_sum = lax.psum(
        (jnp.sum(scaled_gradient, axis=1), jnp.sum(scaled_gradient * standardized_input, axis=1)),
        "row",
    )
    input_gradient = inverse_deviation[:, None] * (
        scaled_gradient
        - first_term_sum[:, None] / feature_width
        - standardized_input * (second_term_sum[:, None] / feature_width)
    )
    return (input_gradient.astype(jnp.bfloat16), gain_gradient, grad_wqkv, grad_wout)

MESH = pl.DeviceIdType.MESH
F32 = jnp.float32
BF16 = jnp.bfloat16
NT = (((1,), (1,)), ((), ()))
TN = (((0,), (0,)), ((), ()))
NN = (((1,), (0,)), ((), ()))


def mm(a, b, dims=NN):
    return lax.dot_general(a, b, dims, preferred_element_type=F32)


def block_kernel(
    chips, x_ref, gain_ref, g_ref, wqkv_hbm, wout_hbm,
    n_out, g_out, ctx_out, dqkv_out, xhat_out, rstd_out, here_out, up_out, down_out, pass_out,
    wqkv, wout, nbuf, gbuf, xhat, rstd_buf, stat_send, stat_recv,
    q_send, q_recv, qkv, probs, ctx, dc_send, dc_recv, dctx, dqkv,
    acc, sib_send, sib_recv, z_send, z_pass, z_recv, total, own_part,
    w_sem, out_sem, ctx_sem, stat_ss, stat_rs, ag_up, ag_down, ag_recv, sib_ss, sib_rs,
    q_ss, q_rs, c_ss, c_rs, dc_ss, dc_rs, dq_ss, dq_rs,
    ps_ss, ps_rs, rs_ss, rs_rs,
):
    row = lax.axis_index("row")
    col = lax.axis_index("col")
    dp = lax.axis_index("dp")
    z = col // 2
    core = col % 2
    rows, width = x_ref.shape
    tokens = nbuf.shape[0]
    own_heads = qkv.shape[0]
    scale = 1.0 / math.sqrt(HS)
    across = (1 - row, col, dp)
    sibling = (row, z * 2 + 1 - core, dp)
    above = (row, jnp.minimum(z + 1, chips - 1) * 2 + core, dp)
    below = (row, jnp.maximum(z - 1, 0) * 2 + core, dp)
    peers = 2 * chips

    barrier = pltpu.get_barrier_semaphore()
    pl.semaphore_signal(barrier, inc=1, device_id=across, device_id_type=MESH)
    for k in range(1, peers):
        pl.semaphore_signal(
            barrier, inc=1, device_id=(row, (col + k) % peers, dp), device_id_type=MESH
        )
    load_qkv = pltpu.make_async_copy(wqkv_hbm, wqkv, w_sem.at[0])
    load_out = pltpu.make_async_copy(wout_hbm, wout, w_sem.at[1])
    load_qkv.start()
    load_out.start()

    x = x_ref[...].astype(F32)
    mean_here = jnp.sum(x, axis=1, keepdims=True) / width
    dev = x - mean_here
    m2_here = jnp.sum(dev * dev, axis=1, keepdims=True)
    stat_send[0, 0] = jnp.broadcast_to(mean_here, (rows, HS))
    stat_send[0, 1] = jnp.broadcast_to(m2_here, (rows, HS))
    gbuf[pl.ds(pl.multiple_of(col * rows, rows), rows), :] = g_ref[...]
    pl.semaphore_wait(barrier, peers)

    def remote(src, dst, ss, rs, device):
        return pltpu.make_async_remote_copy(
            src_ref=src, dst_ref=dst, send_sem=ss, recv_sem=rs, device_id=device, device_id_type=MESH
        )

    def slot(buf, chip, which):
        return buf.at[pl.ds(pl.multiple_of((chip * 2 + which) * rows, rows), rows), :]

    def z_copy(a, buf, b, up):
        here = slot(buf, b, core)
        ss = ag_up if up else ag_down
        return remote(here, here, ss.at[a, b], ag_recv.at[a, b], above if up else below)

    def s_copy(a, buf, b):
        here = slot(buf, b, core)
        return remote(here, here, sib_ss.at[a, b], sib_rs.at[a, b], sibling)

    def gather_step(a, buf, d):
        if d == 0:
            @pl.when(z < chips - 1)
            def _():
                z_copy(a, buf, z, True).start()

            @pl.when(z > 0)
            def _():
                z_copy(a, buf, z, False).start()

            s_copy(a, buf, z).start()
            return

        @pl.when(z >= d)
        def _():
            z_copy(a, buf, z - d, True).wait_recv()

            @pl.when(z < chips - 1)
            def _():
                z_copy(a, buf, z - d, True).start()

            s_copy(a, buf, z - d).start()

        @pl.when(z + d <= chips - 1)
        def _():
            z_copy(a, buf, z + d, False).wait_recv()

            @pl.when(z > 0)
            def _():
                z_copy(a, buf, z + d, False).start()

            s_copy(a, buf, z + d).start()

    def pair_wait(a, buf, b):
        there = slot(buf, b, 1 - core)
        remote(there, there, sib_ss.at[a, b], sib_rs.at[a, b], sibling).wait_recv()

    def gather_drain(a, buf):
        for b in range(chips):
            s_copy(a, buf, b).wait_send()

            @pl.when((b <= z) & (z < chips - 1))
            def _():
                z_copy(a, buf, b, True).wait_send()

            @pl.when((b >= z) & (z > 0))
            def _():
                z_copy(a, buf, b, False).wait_send()

    gather_step(1, gbuf, 0)

    stats = remote(stat_send.at[0], stat_recv.at[0], stat_ss.at[0], stat_rs.at[0], across)
    stats.start()
    stats.wait_recv()
    mean_there = stat_recv[0, 0][:, :1]
    m2_there = stat_recv[0, 1][:, :1]
    gap = mean_here - mean_there
    average = (mean_here + mean_there) * 0.5
    variance = (m2_here + m2_there + gap * gap * (0.5 * width)) / (2.0 * width)
    rstd = lax.rsqrt(variance + EPS)
    rstd_buf[...] = jnp.broadcast_to(rstd, (rows, HS))
    hat = (x_ref[...].astype(F32) - average) * rstd
    xhat[...] = hat
    nbuf[pl.ds(pl.multiple_of(col * rows, rows), rows), :] = (hat * gain_ref[...]).astype(BF16)

    wide = 3 * HS
    deep = 1024
    chip_rows = 2 * rows
    low = z < chips // 2
    near = jnp.where(low, 0, 2)
    third = jnp.where(low, 2, 1)
    last = jnp.where(low, 3, 0)

    def head_cols(r, i):
        return pl.ds(pl.multiple_of((r * own_heads + i) * wide, HS), wide)

    def pieces(k):
        return pl.ds(pl.multiple_of(k * deep, deep), deep)

    def chip_span(b, count):
        return pl.ds(pl.multiple_of(b * chip_rows, chip_rows), count * chip_rows)

    spans = [(chip_span(near, 2), 2 * chip_rows), (chip_span(third, 1), chip_rows), (chip_span(last, 1), chip_rows)]

    def q_copy(i, j):
        here = spans[j][0]
        return remote(q_send.at[i, here], q_recv.at[i, here], q_ss.at[j, i], q_rs.at[j, i], across)

    def project_piece(j):
        here, count = spans[j]

        def project(cols):
            total[0:count] = jnp.zeros((count, wide), F32)

            def step(k, carry):
                total[0:count] += mm(nbuf[here, pieces(k)], wqkv[pieces(k), cols])
                return carry

            lax.fori_loop(0, width // deep, step, 0)

        def there(i, carry):
            project(head_cols(1 - row, i))
            q_send[i, here] = total[0:count].astype(BF16)
            q_copy(i, j).start()
            return carry

        def own(i, carry):
            project(head_cols(row, i))
            own_part[i, here] = total[0:count]
            return carry

        lax.fori_loop(0, own_heads, there, 0)
        lax.fori_loop(0, own_heads, own, 0)

    gather_step(0, nbuf, 0)
    gather_step(0, nbuf, 1)
    load_qkv.wait()
    pair_wait(0, nbuf, near)
    pair_wait(0, nbuf, near + 1)
    project_piece(0)
    gather_step(0, nbuf, 2)
    gather_step(1, gbuf, 1)
    pair_wait(0, nbuf, third)
    project_piece(1)
    gather_step(0, nbuf, 3)
    pair_wait(0, nbuf, last)
    save_n = pltpu.make_async_copy(nbuf, n_out, out_sem.at[0])
    save_n.start()
    project_piece(2)
    gather_step(1, gbuf, 2)

    def join(i, carry):
        for j in range(3):
            q_copy(i, j).wait_recv()
        qkv[i] = (own_part[i] + q_recv[i].astype(F32)).astype(BF16)
        return carry

    lax.fori_loop(0, own_heads, join, 0)

    allowed = lax.broadcasted_iota(jnp.int32, (tokens, tokens), 1) <= lax.broadcasted_iota(
        jnp.int32, (tokens, tokens), 0
    )

    def ctx_copy(i):
        here = ctx.at[row * own_heads + i]
        return remote(here, here, c_ss.at[i], c_rs.at[i], across)

    def forward(i, carry):
        q = qkv[i, :, 0:HS]
        k = qkv[i, :, HS:2 * HS]
        v = qkv[i, :, 2 * HS:3 * HS]
        s = jnp.where(allowed, mm(q, k, NT) * scale, -jnp.inf)
        e = jnp.exp(s - jnp.max(s, axis=1, keepdims=True))
        p = e / jnp.sum(e, axis=1, keepdims=True)
        probs[i] = p
        ctx[row * own_heads + i] = mm(p.astype(BF16), v).astype(BF16)
        ctx_copy(i).start()
        return carry

    lax.fori_loop(0, own_heads, forward, 0)

    load_out.wait()
    span = own_heads * HS
    early = pl.ds(pl.multiple_of(jnp.where(low, 0, chip_rows), chip_rows), 3 * chip_rows)
    parts = [(early, 3 * chip_rows), spans[2]]

    def out_rows(r):
        return pl.ds(pl.multiple_of(r * span, HS), span)

    def context_part(r, here, count):
        total[0:count] = jnp.zeros((count, span), F32)

        def step(k, carry):
            total[0:count] += mm(gbuf[here, pieces(k)], wout[out_rows(r), pieces(k)], NT)
            return carry

        lax.fori_loop(0, width // deep, step, 0)

    dc_copies = []
    for j in range(2):
        here, count = parts[j]
        if j == 0:
            pair_wait(1, gbuf, near)
            pair_wait(1, gbuf, near + 1)
            pair_wait(1, gbuf, third)
        else:
            gather_step(1, gbuf, 3)
            pair_wait(1, gbuf, last)
            save_g = pltpu.make_async_copy(gbuf, g_out, out_sem.at[1])
            save_g.start()
        context_part(1 - row, here, count)
        dc_send[here] = total[0:count].astype(BF16)
        dc_copies.append(remote(dc_send.at[here], dc_recv.at[here], dc_ss.at[j], dc_rs.at[j], across))
        dc_copies[j].start()
        context_part(row, here, count)
        own_part[0, here] = total[0:count]
    for dc_copy in dc_copies:
        dc_copy.wait_recv()
    dc = (own_part[0] + dc_recv[...].astype(F32)).astype(BF16)
    for i in range(own_heads):
        dctx[i] = dc[:, i * HS:(i + 1) * HS]

    def dq_copy(i):
        here = dqkv.at[:, head_cols(row, i)]
        return remote(here, here, dq_ss.at[i], dq_rs.at[i], across)

    def backward(i, carry):
        q = qkv[i, :, 0:HS]
        k = qkv[i, :, HS:2 * HS]
        v = qkv[i, :, 2 * HS:3 * HS]
        p = probs[i]
        dch = dctx[i]
        d_p = mm(dch, v, NT)
        delta = jnp.sum(p * d_p, axis=1, keepdims=True)
        d_s = (p * (d_p - delta) * scale).astype(BF16)
        d_q = mm(d_s, k)
        d_k = mm(d_s, q, TN)
        d_v = mm(p.astype(BF16), dch, TN)
        dqkv[:, head_cols(row, i)] = jnp.concatenate([d_q, d_k, d_v], axis=1).astype(BF16)
        dq_copy(i).start()
        return carry

    lax.fori_loop(0, own_heads, backward, 0)
    tile = 256

    half_cols = own_heads * wide

    def block_rows(b, which, cols):
        return dqkv[pl.ds(pl.multiple_of((b * 2 + which) * rows, rows), rows), cols]

    def stacked(b0, b1, cols):
        order = [(b0, core), (b1, core), (b0, 1 - core), (b1, 1 - core)]
        return jnp.concatenate([block_rows(b, which, cols) for b, which in order], axis=0)

    def row_cols(r):
        return pl.ds(pl.multiple_of(r * half_cols, HS), half_cols)

    def tiled(body):
        def step(t, carry):
            body(pl.ds(pl.multiple_of(t * tile, tile), tile))
            return carry

        lax.fori_loop(0, width // tile, step, 0)

    def keep(b0, b1, cols, out):
        acc[b0, :, cols] = out[0:rows]
        acc[b1, :, cols] = out[rows:2 * rows]
        sib_send[b0, :, cols] = out[2 * rows:3 * rows].astype(BF16)
        sib_send[b1, :, cols] = out[3 * rows:].astype(BF16)

    def pair_copy(b):
        return remote(sib_send.at[b], sib_recv.at[b], ps_ss.at[b], ps_rs.at[b], sibling)

    def line_copy(b, up):
        w = 0 if up else 1
        return remote(z_send, z_recv.at[w], rs_ss.at[w], rs_rs.at[w], above if up else below)

    def hop_far():
        @pl.when(z == 0)
        def _():
            z_send[...] = acc[far].astype(BF16)
            line_copy(far, True).start()

        @pl.when(z == far)
        def _():
            z_send[...] = acc[0].astype(BF16)
            line_copy(0, False).start()

    def add_pair(b):
        pair_copy(b).wait_recv()
        acc[b] = acc[b] + sib_recv[b].astype(F32)

    far = chips - 1
    def own_share(cols):
        out = mm(stacked(0, far, row_cols(row)), wqkv[cols, row_cols(row)], NT)
        for k, b in enumerate((0, far, 1, 2)):
            acc[b, :, cols] = out[k * rows:(k + 1) * rows]

    tiled(own_share)
    for i in range(own_heads):
        there = dqkv.at[:, head_cols(1 - row, i)]
        remote(there, there, dq_ss.at[i], dq_rs.at[i], across).wait_recv()
        other = ctx.at[(1 - row) * own_heads + i]
        remote(other, other, c_ss.at[i], c_rs.at[i], across).wait_recv()
    save_dqkv = pltpu.make_async_copy(dqkv, dqkv_out, out_sem.at[2])
    save_dqkv.start()
    ctx_saves = []
    for h in range(2 * own_heads):
        to = ctx_out.at[:, h * HS:(h + 1) * HS]
        ctx_saves.append(pltpu.make_async_copy(ctx.at[h], to, ctx_sem.at[h]))
        ctx_saves[h].start()

    def other_share(cols):
        out = mm(stacked(0, far, row_cols(1 - row)), wqkv[cols, row_cols(1 - row)], NT)
        before = jnp.concatenate([acc[b, :, cols] for b in (0, far, 1, 2)], axis=0)
        keep(0, far, cols, out + before)

    tiled(other_share)
    for b in (0, far):
        pair_copy(b).start()
    add_pair(0)
    add_pair(far)
    hop_far()

    def both_shares(cols):
        every = slice(None)
        keep(1, 2, cols, mm(stacked(1, 2, every), wqkv[cols, :], NT))

    tiled(both_shares)
    for b in (1, 2):
        pair_copy(b).start()
    add_pair(1)
    add_pair(2)

    half = chips // 2
    b_pass = jnp.where(z < half, z + half, z - half)
    z_pass[...] = acc[b_pass].astype(BF16)

    @pl.when(z == 1)
    def _():
        line_copy(far, True).wait_recv()
        z_pass[...] = (acc[far] + z_recv[0].astype(F32)).astype(BF16)

    @pl.when(z == far - 1)
    def _():
        line_copy(0, False).wait_recv()
        z_pass[...] = (acc[0] + z_recv[1].astype(F32)).astype(BF16)

    saves = [
        pltpu.make_async_copy(xhat, xhat_out, out_sem.at[4]),
        pltpu.make_async_copy(rstd_buf, rstd_out, out_sem.at[5]),
        pltpu.make_async_copy(acc.at[z], here_out, out_sem.at[6]),
        pltpu.make_async_copy(acc.at[jnp.minimum(z + 1, far)], up_out, out_sem.at[7]),
        pltpu.make_async_copy(acc.at[jnp.maximum(z - 1, 0)], down_out, out_sem.at[8]),
        pltpu.make_async_copy(z_pass, pass_out, out_sem.at[9]),
    ]
    for save in saves:
        save.start()

    stats.wait_send()
    gather_drain(0, nbuf)
    gather_drain(1, gbuf)
    for i in range(own_heads):
        for j in range(3):
            q_copy(i, j).wait_send()
        ctx_copy(i).wait_send()
        dq_copy(i).wait_send()
    for dc_copy in dc_copies:
        dc_copy.wait_send()
    for b in range(chips):
        pair_copy(b).wait_send()

    @pl.when(z == 0)
    def _():
        line_copy(far, True).wait_send()

    @pl.when(z == far)
    def _():
        line_copy(0, False).wait_send()

    save_n.wait()
    save_g.wait()
    save_dqkv.wait()
    for save in saves:
        save.wait()
    for save in ctx_saves:
        save.wait()


def norm_kernel(
    here_ref, from_below, from_above, xhat_ref, rstd_ref, gain_ref, dx_ref, dgain_ref,
    dn_buf, stat_send, stat_recv, gg_send, gg_recv, stat_ss, stat_rs, gg_ss, gg_rs,
):
    row = lax.axis_index("row")
    col = lax.axis_index("col")
    dp = lax.axis_index("dp")
    rows, width = here_ref.shape
    peers = gg_recv.shape[0]
    across = (1 - row, col, dp)

    barrier = pltpu.get_barrier_semaphore()
    pl.semaphore_signal(barrier, inc=1, device_id=across, device_id_type=MESH)
    for k in range(1, peers):
        pl.semaphore_signal(
            barrier, inc=1, device_id=(row, (col + k) % peers, dp), device_id_type=MESH
        )
    dn = here_ref[...] + from_below[...].astype(F32) + from_above[...].astype(F32)
    sg = dn * gain_ref[...]
    dn_buf[...] = sg
    hat = xhat_ref[...]
    first = jnp.sum(sg, axis=1, keepdims=True)
    second = jnp.sum(sg * hat, axis=1, keepdims=True)
    stat_send[0] = jnp.broadcast_to(first, (rows, HS))
    stat_send[1] = jnp.broadcast_to(second, (rows, HS))
    gg_send[...] = jnp.sum(dn * hat, axis=0, keepdims=True)
    pl.semaphore_wait(barrier, peers)

    stats = pltpu.make_async_remote_copy(
        src_ref=stat_send, dst_ref=stat_recv, send_sem=stat_ss.at[0], recv_sem=stat_rs.at[0],
        device_id=across, device_id_type=MESH,
    )
    stats.start()

    def gg_copy(k, source):
        return pltpu.make_async_remote_copy(
            src_ref=gg_send, dst_ref=gg_recv.at[source], send_sem=gg_ss.at[k], recv_sem=gg_rs.at[source],
            device_id=(row, (col + k) % peers, dp), device_id_type=MESH,
        )

    for k in range(1, peers):
        gg_copy(k, col).start()
    stats.wait_recv()
    first = (first + stat_recv[0][:, :1]) / (2.0 * width)
    second = (second + stat_recv[1][:, :1]) / (2.0 * width)
    dx_ref[...] = (rstd_ref[:, :1] * (dn_buf[...] - first - xhat_ref[...] * second)).astype(BF16)
    gg_recv[col] = gg_send[...]
    for k in range(1, peers):
        gg_copy(k, (col + k) % peers).wait_recv()
    whole = gg_recv[0]
    for k in range(1, peers):
        whole = whole + gg_recv[k]
    dgain_ref[...] = whole
    stats.wait_send()
    for k in range(1, peers):
        gg_copy(k, col).wait_send()


def weight_gradient(left, right, tile, wide):
    tokens, height = left.shape
    columns = right.shape[1]

    def kernel(left_ref, right_ref, out_ref):
        turned = left_ref[...].T
        for at in range(0, columns, wide):
            out_ref[:, at:at + wide] = mm(turned, right_ref[:, at:at + wide]).astype(BF16)

    return pl.pallas_call(
        kernel,
        grid=(height // tile,),
        out_shape=jax.ShapeDtypeStruct((height, columns), BF16),
        in_specs=[
            pl.BlockSpec((tokens, tile), lambda i: (0, i)),
            pl.BlockSpec((tokens, columns), lambda i: (0, 0)),
        ],
        out_specs=pl.BlockSpec((tile, columns), lambda i: (i, 0)),
        compiler_params=pltpu.CompilerParams(vmem_limit_bytes=32 * 2**20),
        cost_estimate=pl.CostEstimate(
            flops=2 * tokens * height * columns,
            bytes_accessed=2 * (tokens * (height + columns) + height * columns),
            transcendentals=0,
        ),
    )(left, right)


def pair_shards(layer_input, layer_norm_gain, w_qkv, w_out, out_grad):
    rows, width = layer_input.shape
    peers = lax.axis_size("col")
    chips = peers // 2
    tokens = rows * peers
    columns = w_qkv.shape[1]
    heads = columns // (3 * HS)
    own = heads // 2
    vmem = pl.BlockSpec(memory_space=pltpu.VMEM)
    hbm = pl.BlockSpec(memory_space=pl.ANY)
    dma = pltpu.SemaphoreType.DMA
    shape = jax.ShapeDtypeStruct
    normed, grad, context, dqkv, xhat, rstd, here, up, down, onward = pl.pallas_call(
        functools.partial(block_kernel, chips),
        out_shape=[
            shape((tokens, width), BF16),
            shape((tokens, width), BF16),
            shape((tokens, heads * HS), BF16),
            shape((tokens, columns), BF16),
            shape((rows, width), F32),
            shape((rows, HS), F32),
            shape((rows, width), F32),
            shape((rows, width), F32),
            shape((rows, width), F32),
            shape((rows, width), BF16),
        ],
        in_specs=[vmem, vmem, vmem, hbm, hbm],
        out_specs=[hbm] * 10,
        scratch_shapes=[
            pltpu.VMEM(w_qkv.shape, BF16),
            pltpu.VMEM(w_out.shape, BF16),
            pltpu.VMEM((tokens, width), BF16),
            pltpu.VMEM((tokens, width), BF16),
            pltpu.VMEM((rows, width), F32),
            pltpu.VMEM((rows, HS), F32),
            pltpu.VMEM((1, 2, rows, HS), F32),
            pltpu.VMEM((1, 2, rows, HS), F32),
            pltpu.VMEM((own, tokens, 3 * HS), BF16),
            pltpu.VMEM((own, tokens, 3 * HS), BF16),
            pltpu.VMEM((own, tokens, 3 * HS), BF16),
            pltpu.VMEM((own, tokens, tokens), F32),
            pltpu.VMEM((heads, tokens, HS), BF16),
            pltpu.VMEM((tokens, own * HS), BF16),
            pltpu.VMEM((tokens, own * HS), BF16),
            pltpu.VMEM((own, tokens, HS), BF16),
            pltpu.VMEM((tokens, columns), BF16),
            pltpu.VMEM((chips, rows, width), F32),
            pltpu.VMEM((chips, rows, width), BF16),
            pltpu.VMEM((chips, rows, width), BF16),
            pltpu.VMEM((rows, width), BF16),
            pltpu.VMEM((rows, width), BF16),
            pltpu.VMEM((2, rows, width), BF16),
            pltpu.VMEM((tokens, 3 * HS), F32),
            pltpu.VMEM((own, tokens, 3 * HS), F32),
            dma((2,)), dma((10,)), dma((heads,)), dma((1,)), dma((1,)),
            dma((2, chips)), dma((2, chips)), dma((2, chips)), dma((2, chips)), dma((2, chips)),
            dma((3, own)), dma((3, own)), dma((own,)), dma((own,)),
            dma((2,)), dma((2,)), dma((own,)), dma((own,)),
            dma((chips,)), dma((chips,)), dma((2,)), dma((2,)),
        ],
        compiler_params=pltpu.CompilerParams(
            collective_id=0, has_side_effects=True, vmem_limit_bytes=63 * 2**20
        ),
    )(layer_input, layer_norm_gain.reshape(1, width), out_grad, w_qkv, w_out)
    half = chips // 2
    both = range(2)
    rise = [(2 * z + c, 2 * z + 2 + c) for z in range(chips - 1) for c in both]
    fall = [(b, a) for a, b in rise]
    rise_first = [(2 * z + c, 2 * z + 2 + c) for z in range(half) for c in both]
    fall_first = [(2 * z + c, 2 * z - 2 + c) for z in range(half, chips) for c in both]
    got_up = lax.ppermute(onward, "col", rise_first)
    got_down = lax.ppermute(onward, "col", fall_first)
    grad_wqkv = weight_gradient(normed, dqkv, 512, 3 * HS)
    got_up, got_down, grad_wqkv = lax.optimization_barrier((got_up, got_down, grad_wqkv))
    next_up = (up + got_up.astype(F32)).astype(BF16)
    next_down = (down + got_down.astype(F32)).astype(BF16)
    from_below = lax.ppermute(next_up, "col", rise)
    from_above = lax.ppermute(next_down, "col", fall)
    grad_wout = weight_gradient(context, grad, HS, 4 * HS)
    dx, dgain = pl.pallas_call(
        norm_kernel,
        out_shape=[shape((rows, width), BF16), shape((1, width), F32)],
        in_specs=[vmem] * 6,
        out_specs=[vmem] * 2,
        scratch_shapes=[
            pltpu.VMEM((rows, width), F32),
            pltpu.VMEM((2, rows, HS), F32),
            pltpu.VMEM((2, rows, HS), F32),
            pltpu.VMEM((1, width), F32),
            pltpu.VMEM((peers, 1, width), F32),
            dma((1,)), dma((1,)), dma((peers,)), dma((peers,)),
        ],
        compiler_params=pltpu.CompilerParams(
            collective_id=1, has_side_effects=True, vmem_limit_bytes=24 * 2**20
        ),
    )(here, from_below, from_above, xhat, rstd, layer_norm_gain.reshape(1, width))
    return dx, dgain.reshape(width), grad_wqkv, grad_wout


def choose(layer_input, layer_norm_gain, w_qkv, w_out, out_grad):
    paired = lax.axis_size("row") == 2 and lax.axis_size("col") == 8
    sized = layer_input.shape[1] % 1024 == 0 and layer_input.shape[0] == 32
    body = pair_shards if paired and sized and w_qkv.shape[1] == 18 * HS else shards
    return body(layer_input, layer_norm_gain, w_qkv, w_out, out_grad)


def solution(mesh):
    in_specs = (
        P(("dp", "col"), "row"),
        P("row"),
        P("row", "col"),
        P("col", "row"),
        P(("dp", "col"), "row"),
    )
    out_specs = (
        P(("dp", "col"), "row"),
        P(("dp", "row")),
        P(("dp", "row"), "col"),
        P(("dp", "col"), "row"),
    )
    return jax.shard_map(choose, mesh=mesh, in_specs=in_specs, out_specs=out_specs, check_vma=False)
```

```python
import functools
import math

import jax
import jax.numpy as jnp
from jax import lax
from jax.experimental import pallas as pl
from jax.experimental.pallas import tpu as pltpu
from jax.sharding import PartitionSpec as P

HS = 128


EPS = 1e-05


def shards(layer_input, layer_norm_gain, w_qkv, w_out, out_grad):
    rows_here, features_here = layer_input.shape
    col_count = lax.axis_size("col")
    row_count = lax.axis_size("row")
    tokens = rows_here * col_count
    tok_row = tokens // row_count
    feature_width = features_here * row_count
    heads_here = w_qkv.shape[1] // (3 * HS)
    scale = 1.0 / math.sqrt(HS)
    input_float = layer_input.astype(jnp.float32)
    average = lax.psum(jnp.sum(input_float, axis=1), "row") / feature_width
    centered_input = input_float - average[:, None]
    variance = lax.psum(jnp.sum(centered_input * centered_input, axis=1), "row") / feature_width
    inverse_deviation = lax.rsqrt(variance + EPS)
    standardized_input = centered_input * inverse_deviation[:, None]
    normalized_output = (standardized_input * layer_norm_gain[None, :]).astype(jnp.bfloat16)
    normed_all = lax.all_gather(normalized_output, "col", axis=0, tiled=True)
    first_query = lax.axis_index("row") * tok_row
    piece = normed_all
    owned = lax.psum_scatter(
        jnp.dot(piece, w_qkv, preferred_element_type=jnp.float32),
        "row",
        scatter_dimension=0,
        tiled=True,
    ).astype(jnp.bfloat16)
    owned = owned.reshape(tok_row, heads_here, 3, HS)
    query = owned[:, :, 0]
    key_value = lax.all_gather(owned[:, :, 1:], "row", axis=0, tiled=True)
    keys = key_value[:, :, 0]
    values = key_value[:, :, 1]
    query_pos = first_query + jnp.arange(tok_row)
    key_pos = jnp.arange(tokens)
    allowed = key_pos[None, :] <= query_pos[:, None]
    scores = jnp.einsum("qhe,khe->hqk", query, keys, preferred_element_type=jnp.float32) * scale
    scores = jnp.where(allowed[None], scores, -jnp.inf)
    highest = jnp.max(scores, axis=2, keepdims=True)
    powers = jnp.exp(scores - highest)
    totals = jnp.sum(powers, axis=2, keepdims=True)
    probs = powers / totals
    probs_b = probs.astype(jnp.bfloat16)
    context = jnp.einsum(
        "hqk,khe->qhe", probs_b, values, preferred_element_type=jnp.float32
    ).astype(jnp.bfloat16)
    context_all = lax.all_gather(
        context.reshape(tok_row, heads_here * HS), "row", axis=0, tiled=True
    )
    grad_all = lax.all_gather(out_grad, "col", axis=0, tiled=True)
    grad_wout = lax.dot_general(
        context_all, grad_all, (((0,), (0,)), ((), ())), preferred_element_type=jnp.float32
    ).astype(jnp.bfloat16)
    piece = grad_all
    d_context = lax.psum_scatter(
        lax.dot_general(piece, w_out, (((1,), (1,)), ((), ())), preferred_element_type=jnp.float32),
        "row",
        scatter_dimension=0,
        tiled=True,
    ).astype(jnp.bfloat16)
    d_context = d_context.reshape(tok_row, heads_here, HS)
    d_probs = jnp.einsum("qhe,khe->hqk", d_context, values, preferred_element_type=jnp.float32)
    delta = jnp.sum(probs * d_probs, axis=2, keepdims=True)
    d_scores = (probs * (d_probs - delta) * scale).astype(jnp.bfloat16)
    d_query = jnp.einsum("hqk,khe->qhe", d_scores, keys, preferred_element_type=jnp.float32).astype(
        jnp.bfloat16
    )
    d_keys = jnp.einsum("hqk,qhe->khe", d_scores, query, preferred_element_type=jnp.float32)
    d_values = jnp.einsum("hqk,qhe->khe", probs_b, d_context, preferred_element_type=jnp.float32)
    d_pairs = jnp.stack([d_keys, d_values], axis=2)
    pair_owned = lax.psum_scatter(d_pairs, "row", scatter_dimension=0, tiled=True).astype(
        jnp.bfloat16
    )
    owned_grad = jnp.concatenate([d_query[:, :, None], pair_owned], axis=2)
    owned_grad = owned_grad.reshape(tok_row, heads_here * 3 * HS)
    d_qkv_all = lax.all_gather(owned_grad, "row", axis=0, tiled=True)
    grad_wqkv = lax.dot_general(
        normed_all, d_qkv_all, (((0,), (0,)), ((), ())), preferred_element_type=jnp.float32
    ).astype(jnp.bfloat16)
    piece = d_qkv_all
    normalized_gradient = lax.psum_scatter(
        lax.dot_general(piece, w_qkv, (((1,), (1,)), ((), ())), preferred_element_type=jnp.float32),
        "col",
        scatter_dimension=0,
        tiled=True,
    )
    gain_gradient = lax.psum(jnp.sum(normalized_gradient * standardized_input, axis=0), "col")
    scaled_gradient = normalized_gradient * layer_norm_gain[None, :]
    first_term_sum, second_term_sum = lax.psum(
        (jnp.sum(scaled_gradient, axis=1), jnp.sum(scaled_gradient * standardized_input, axis=1)),
        "row",
    )
    input_gradient = inverse_deviation[:, None] * (
        scaled_gradient
        - first_term_sum[:, None] / feature_width
        - standardized_input * (second_term_sum[:, None] / feature_width)
    )
    return (input_gradient.astype(jnp.bfloat16), gain_gradient, grad_wqkv, grad_wout)

MESH = pl.DeviceIdType.MESH
F32 = jnp.float32
BF16 = jnp.bfloat16
NT = (((1,), (1,)), ((), ()))
TN = (((0,), (0,)), ((), ()))
NN = (((1,), (0,)), ((), ()))


def mm(a, b, dims=NN):
    return lax.dot_general(a, b, dims, preferred_element_type=F32)


def block_kernel(
    chips, x_ref, gain_ref, g_ref, wqkv_hbm, wout_hbm,
    n_out, g_out, ctx_out, dqkv_out, xhat_out, rstd_out, here_out, up_out, down_out, pass_out,
    wqkv, wout, nbuf, gbuf, xhat, rstd_buf, stat_send, stat_recv,
    q_send, q_recv, qkv, probs, ctx, dc_send, dc_recv, dctx, dqkv,
    acc, sib_send, sib_recv, z_send, z_pass, z_recv, total, own_part,
    w_sem, out_sem, ctx_sem, stat_ss, stat_rs, ag_up, ag_down, ag_recv, sib_ss, sib_rs,
    q_ss, q_rs, c_ss, c_rs, dc_ss, dc_rs, dq_ss, dq_rs,
    ps_ss, ps_rs, rs_ss, rs_rs,
):
    row = lax.axis_index("row")
    col = lax.axis_index("col")
    dp = lax.axis_index("dp")
    z = col // 2
    core = col % 2
    rows, width = x_ref.shape
    tokens = nbuf.shape[0]
    own_heads = qkv.shape[0]
    scale = 1.0 / math.sqrt(HS)
    across = (1 - row, col, dp)
    sibling = (row, z * 2 + 1 - core, dp)
    above = (row, jnp.minimum(z + 1, chips - 1) * 2 + core, dp)
    below = (row, jnp.maximum(z - 1, 0) * 2 + core, dp)
    peers = 2 * chips

    barrier = pltpu.get_barrier_semaphore()
    pl.semaphore_signal(barrier, inc=1, device_id=across, device_id_type=MESH)
    for k in range(1, peers):
        pl.semaphore_signal(
            barrier, inc=1, device_id=(row, (col + k) % peers, dp), device_id_type=MESH
        )
    load_qkv = pltpu.make_async_copy(wqkv_hbm, wqkv, w_sem.at[0])
    load_out = pltpu.make_async_copy(wout_hbm, wout, w_sem.at[1])
    load_qkv.start()
    load_out.start()

    x = x_ref[...].astype(F32)
    mean_here = jnp.sum(x, axis=1, keepdims=True) / width
    dev = x - mean_here
    m2_here = jnp.sum(dev * dev, axis=1, keepdims=True)
    stat_send[0, 0] = jnp.broadcast_to(mean_here, (rows, HS))
    stat_send[0, 1] = jnp.broadcast_to(m2_here, (rows, HS))
    gbuf[pl.ds(pl.multiple_of(col * rows, rows), rows), :] = g_ref[...]
    pl.semaphore_wait(barrier, peers)

    def remote(src, dst, ss, rs, device):
        return pltpu.make_async_remote_copy(
            src_ref=src, dst_ref=dst, send_sem=ss, recv_sem=rs, device_id=device, device_id_type=MESH
        )

    def slot(buf, chip, which):
        return buf.at[pl.ds(pl.multiple_of((chip * 2 + which) * rows, rows), rows), :]

    def z_copy(a, buf, b, up):
        here = slot(buf, b, core)
        ss = ag_up if up else ag_down
        return remote(here, here, ss.at[a, b], ag_recv.at[a, b], above if up else below)

    def s_copy(a, buf, b):
        here = slot(buf, b, core)
        return remote(here, here, sib_ss.at[a, b], sib_rs.at[a, b], sibling)

    def gather_step(a, buf, d):
        if d == 0:
            @pl.when(z < chips - 1)
            def _():
                z_copy(a, buf, z, True).start()

            @pl.when(z > 0)
            def _():
                z_copy(a, buf, z, False).start()

            s_copy(a, buf, z).start()
            return

        @pl.when(z >= d)
        def _():
            z_copy(a, buf, z - d, True).wait_recv()

            @pl.when(z < chips - 1)
            def _():
                z_copy(a, buf, z - d, True).start()

            s_copy(a, buf, z - d).start()

        @pl.when(z + d <= chips - 1)
        def _():
            z_copy(a, buf, z + d, False).wait_recv()

            @pl.when(z > 0)
            def _():
                z_copy(a, buf, z + d, False).start()

            s_copy(a, buf, z + d).start()

    def pair_wait(a, buf, b):
        there = slot(buf, b, 1 - core)
        remote(there, there, sib_ss.at[a, b], sib_rs.at[a, b], sibling).wait_recv()

    def gather_drain(a, buf):
        for b in range(chips):
            s_copy(a, buf, b).wait_send()

            @pl.when((b <= z) & (z < chips - 1))
            def _():
                z_copy(a, buf, b, True).wait_send()

            @pl.when((b >= z) & (z > 0))
            def _():
                z_copy(a, buf, b, False).wait_send()

    gather_step(1, gbuf, 0)

    stats = remote(stat_send.at[0], stat_recv.at[0], stat_ss.at[0], stat_rs.at[0], across)
    stats.start()
    stats.wait_recv()
    mean_there = stat_recv[0, 0][:, :1]
    m2_there = stat_recv[0, 1][:, :1]
    gap = mean_here - mean_there
    average = (mean_here + mean_there) * 0.5
    variance = (m2_here + m2_there + gap * gap * (0.5 * width)) / (2.0 * width)
    rstd = lax.rsqrt(variance + EPS)
    rstd_buf[...] = jnp.broadcast_to(rstd, (rows, HS))
    hat = (x_ref[...].astype(F32) - average) * rstd
    xhat[...] = hat
    nbuf[pl.ds(pl.multiple_of(col * rows, rows), rows), :] = (hat * gain_ref[...]).astype(BF16)

    wide = 3 * HS
    deep = 1024
    chip_rows = 2 * rows
    low = z < chips // 2
    near = jnp.where(low, 0, 2)
    third = jnp.where(low, 2, 1)
    last = jnp.where(low, 3, 0)

    def head_cols(r, i):
        return pl.ds(pl.multiple_of((r * own_heads + i) * wide, HS), wide)

    def pieces(k):
        return pl.ds(pl.multiple_of(k * deep, deep), deep)

    def chip_span(b, count):
        return pl.ds(pl.multiple_of(b * chip_rows, chip_rows), count * chip_rows)

    spans = [(chip_span(near, 2), 2 * chip_rows), (chip_span(third, 1), chip_rows), (chip_span(last, 1), chip_rows)]

    def q_copy(i, j):
        here = spans[j][0]
        return remote(q_send.at[i, here], q_recv.at[i, here], q_ss.at[j, i], q_rs.at[j, i], across)

    def project_piece(j):
        here, count = spans[j]

        def project(cols):
            total[0:count] = jnp.zeros((count, wide), F32)

            def step(k, carry):
                total[0:count] += mm(nbuf[here, pieces(k)], wqkv[pieces(k), cols])
                return carry

            lax.fori_loop(0, width // deep, step, 0)

        def there(i, carry):
            project(head_cols(1 - row, i))
            q_send[i, here] = total[0:count].astype(BF16)
            q_copy(i, j).start()
            return carry

        def own(i, carry):
            project(head_cols(row, i))
            own_part[i, here] = total[0:count]
            return carry

        lax.fori_loop(0, own_heads, there, 0)
        lax.fori_loop(0, own_heads, own, 0)

    gather_step(0, nbuf, 0)
    gather_step(0, nbuf, 1)
    load_qkv.wait()
    pair_wait(0, nbuf, near)
    pair_wait(0, nbuf, near + 1)
    project_piece(0)
    gather_step(0, nbuf, 2)
    gather_step(1, gbuf, 1)
    pair_wait(0, nbuf, third)
    project_piece(1)
    gather_step(0, nbuf, 3)
    pair_wait(0, nbuf, last)
    save_n = pltpu.make_async_copy(nbuf, n_out, out_sem.at[0])
    save_n.start()
    project_piece(2)
    gather_step(1, gbuf, 2)

    def join(i, carry):
        for j in range(3):
            q_copy(i, j).wait_recv()
        qkv[i] = (own_part[i] + q_recv[i].astype(F32)).astype(BF16)
        return carry

    lax.fori_loop(0, own_heads, join, 0)

    allowed = lax.broadcasted_iota(jnp.int32, (tokens, tokens), 1) <= lax.broadcasted_iota(
        jnp.int32, (tokens, tokens), 0
    )

    def ctx_copy(i):
        here = ctx.at[row * own_heads + i]
        return remote(here, here, c_ss.at[i], c_rs.at[i], across)

    def forward(i, carry):
        q = qkv[i, :, 0:HS]
        k = qkv[i, :, HS:2 * HS]
        v = qkv[i, :, 2 * HS:3 * HS]
        s = jnp.where(allowed, mm(q, k, NT) * scale, -jnp.inf)
        e = jnp.exp(s - jnp.max(s, axis=1, keepdims=True))
        p = e / jnp.sum(e, axis=1, keepdims=True)
        probs[i] = p
        ctx[row * own_heads + i] = mm(p.astype(BF16), v).astype(BF16)
        ctx_copy(i).start()
        return carry

    lax.fori_loop(0, own_heads, forward, 0)

    load_out.wait()
    span = own_heads * HS
    early = pl.ds(pl.multiple_of(jnp.where(low, 0, chip_rows), chip_rows), 3 * chip_rows)
    parts = [(early, 3 * chip_rows), spans[2]]

    def out_rows(r):
        return pl.ds(pl.multiple_of(r * span, HS), span)

    def context_part(r, here, count):
        total[0:count] = jnp.zeros((count, span), F32)

        def step(k, carry):
            total[0:count] += mm(gbuf[here, pieces(k)], wout[out_rows(r), pieces(k)], NT)
            return carry

        lax.fori_loop(0, width // deep, step, 0)

    dc_copies = []
    for j in range(2):
        here, count = parts[j]
        if j == 0:
            pair_wait(1, gbuf, near)
            pair_wait(1, gbuf, near + 1)
            pair_wait(1, gbuf, third)
        else:
            gather_step(1, gbuf, 3)
            pair_wait(1, gbuf, last)
            save_g = pltpu.make_async_copy(gbuf, g_out, out_sem.at[1])
            save_g.start()
        context_part(1 - row, here, count)
        dc_send[here] = total[0:count].astype(BF16)
        dc_copies.append(remote(dc_send.at[here], dc_recv.at[here], dc_ss.at[j], dc_rs.at[j], across))
        dc_copies[j].start()
        context_part(row, here, count)
        own_part[0, here] = total[0:count]
    for dc_copy in dc_copies:
        dc_copy.wait_recv()
    dc = (own_part[0] + dc_recv[...].astype(F32)).astype(BF16)
    for i in range(own_heads):
        dctx[i] = dc[:, i * HS:(i + 1) * HS]

    def dq_copy(i):
        here = dqkv.at[:, head_cols(row, i)]
        return remote(here, here, dq_ss.at[i], dq_rs.at[i], across)

    def backward(i, carry):
        q = qkv[i, :, 0:HS]
        k = qkv[i, :, HS:2 * HS]
        v = qkv[i, :, 2 * HS:3 * HS]
        p = probs[i]
        dch = dctx[i]
        d_p = mm(dch, v, NT)
        delta = jnp.sum(p * d_p, axis=1, keepdims=True)
        d_s = (p * (d_p - delta) * scale).astype(BF16)
        d_q = mm(d_s, k)
        d_k = mm(d_s, q, TN)
        d_v = mm(p.astype(BF16), dch, TN)
        dqkv[:, head_cols(row, i)] = jnp.concatenate([d_q, d_k, d_v], axis=1).astype(BF16)
        dq_copy(i).start()
        return carry

    lax.fori_loop(0, own_heads, backward, 0)
    tile = 256

    half_cols = own_heads * wide

    def block_rows(b, which, cols):
        return dqkv[pl.ds(pl.multiple_of((b * 2 + which) * rows, rows), rows), cols]

    def stacked(b0, b1, cols):
        order = [(b0, core), (b1, core), (b0, 1 - core), (b1, 1 - core)]
        return jnp.concatenate([block_rows(b, which, cols) for b, which in order], axis=0)

    def row_cols(r):
        return pl.ds(pl.multiple_of(r * half_cols, HS), half_cols)

    def tiled(body):
        def step(t, carry):
            body(pl.ds(pl.multiple_of(t * tile, tile), tile))
            return carry

        lax.fori_loop(0, width // tile, step, 0)

    def keep(b0, b1, cols, out):
        acc[b0, :, cols] = out[0:rows]
        acc[b1, :, cols] = out[rows:2 * rows]
        sib_send[b0, :, cols] = out[2 * rows:3 * rows].astype(BF16)
        sib_send[b1, :, cols] = out[3 * rows:].astype(BF16)

    def pair_copy(b):
        return remote(sib_send.at[b], sib_recv.at[b], ps_ss.at[b], ps_rs.at[b], sibling)

    def line_copy(b, up):
        w = 0 if up else 1
        return remote(z_send, z_recv.at[w], rs_ss.at[w], rs_rs.at[w], above if up else below)

    def hop_far():
        @pl.when(z == 0)
        def _():
            z_send[...] = acc[far].astype(BF16)
            line_copy(far, True).start()

        @pl.when(z == far)
        def _():
            z_send[...] = acc[0].astype(BF16)
            line_copy(0, False).start()

    def add_pair(b):
        pair_copy(b).wait_recv()
        acc[b] = acc[b] + sib_recv[b].astype(F32)

    far = chips - 1
    def own_share(cols):
        out = mm(stacked(0, far, row_cols(row)), wqkv[cols, row_cols(row)], NT)
        for k, b in enumerate((0, far, 1, 2)):
            acc[b, :, cols] = out[k * rows:(k + 1) * rows]

    tiled(own_share)
    for i in range(own_heads):
        there = dqkv.at[:, head_cols(1 - row, i)]
        remote(there, there, dq_ss.at[i], dq_rs.at[i], across).wait_recv()
        other = ctx.at[(1 - row) * own_heads + i]
        remote(other, other, c_ss.at[i], c_rs.at[i], across).wait_recv()
    save_dqkv = pltpu.make_async_copy(dqkv, dqkv_out, out_sem.at[2])
    save_dqkv.start()
    ctx_saves = []
    for h in range(2 * own_heads):
        to = ctx_out.at[:, h * HS:(h + 1) * HS]
        ctx_saves.append(pltpu.make_async_copy(ctx.at[h], to, ctx_sem.at[h]))
        ctx_saves[h].start()

    def other_share(cols):
        out = mm(stacked(0, far, row_cols(1 - row)), wqkv[cols, row_cols(1 - row)], NT)
        before = jnp.concatenate([acc[b, :, cols] for b in (0, far, 1, 2)], axis=0)
        keep(0, far, cols, out + before)

    tiled(other_share)
    for b in (0, far):
        pair_copy(b).start()
    add_pair(0)
    add_pair(far)
    hop_far()

    def both_shares(cols):
        every = slice(None)
        keep(1, 2, cols, mm(stacked(1, 2, every), wqkv[cols, :], NT))

    tiled(both_shares)
    for b in (1, 2):
        pair_copy(b).start()
    add_pair(1)
    add_pair(2)

    half = chips // 2
    b_pass = jnp.where(z < half, z + half, z - half)
    z_pass[...] = acc[b_pass].astype(BF16)

    @pl.when(z == 1)
    def _():
        line_copy(far, True).wait_recv()
        z_pass[...] = (acc[far] + z_recv[0].astype(F32)).astype(BF16)

    @pl.when(z == far - 1)
    def _():
        line_copy(0, False).wait_recv()
        z_pass[...] = (acc[0] + z_recv[1].astype(F32)).astype(BF16)

    saves = [
        pltpu.make_async_copy(xhat, xhat_out, out_sem.at[4]),
        pltpu.make_async_copy(rstd_buf, rstd_out, out_sem.at[5]),
        pltpu.make_async_copy(acc.at[z], here_out, out_sem.at[6]),
        pltpu.make_async_copy(acc.at[jnp.minimum(z + 1, far)], up_out, out_sem.at[7]),
        pltpu.make_async_copy(acc.at[jnp.maximum(z - 1, 0)], down_out, out_sem.at[8]),
        pltpu.make_async_copy(z_pass, pass_out, out_sem.at[9]),
    ]
    for save in saves:
        save.start()

    stats.wait_send()
    gather_drain(0, nbuf)
    gather_drain(1, gbuf)
    for i in range(own_heads):
        for j in range(3):
            q_copy(i, j).wait_send()
        ctx_copy(i).wait_send()
        dq_copy(i).wait_send()
    for dc_copy in dc_copies:
        dc_copy.wait_send()
    for b in range(chips):
        pair_copy(b).wait_send()

    @pl.when(z == 0)
    def _():
        line_copy(far, True).wait_send()

    @pl.when(z == far)
    def _():
        line_copy(0, False).wait_send()

    save_n.wait()
    save_g.wait()
    save_dqkv.wait()
    for save in saves:
        save.wait()
    for save in ctx_saves:
        save.wait()


def norm_kernel(
    here_ref, from_below, from_above, xhat_ref, rstd_ref, gain_ref, dx_ref, dgain_ref,
    dn_buf, stat_send, stat_recv, gg_send, gg_recv, stat_ss, stat_rs, gg_ss, gg_rs,
):
    row = lax.axis_index("row")
    col = lax.axis_index("col")
    dp = lax.axis_index("dp")
    rows, width = here_ref.shape
    peers = gg_recv.shape[0]
    across = (1 - row, col, dp)

    barrier = pltpu.get_barrier_semaphore()
    pl.semaphore_signal(barrier, inc=1, device_id=across, device_id_type=MESH)
    for k in range(1, peers):
        pl.semaphore_signal(
            barrier, inc=1, device_id=(row, (col + k) % peers, dp), device_id_type=MESH
        )
    dn = here_ref[...] + from_below[...].astype(F32) + from_above[...].astype(F32)
    sg = dn * gain_ref[...]
    dn_buf[...] = sg
    hat = xhat_ref[...]
    first = jnp.sum(sg, axis=1, keepdims=True)
    second = jnp.sum(sg * hat, axis=1, keepdims=True)
    stat_send[0] = jnp.broadcast_to(first, (rows, HS))
    stat_send[1] = jnp.broadcast_to(second, (rows, HS))
    gg_send[...] = jnp.sum(dn * hat, axis=0, keepdims=True)
    pl.semaphore_wait(barrier, peers)

    stats = pltpu.make_async_remote_copy(
        src_ref=stat_send, dst_ref=stat_recv, send_sem=stat_ss.at[0], recv_sem=stat_rs.at[0],
        device_id=across, device_id_type=MESH,
    )
    stats.start()

    def gg_copy(k, source):
        return pltpu.make_async_remote_copy(
            src_ref=gg_send, dst_ref=gg_recv.at[source], send_sem=gg_ss.at[k], recv_sem=gg_rs.at[source],
            device_id=(row, (col + k) % peers, dp), device_id_type=MESH,
        )

    for k in range(1, peers):
        gg_copy(k, col).start()
    stats.wait_recv()
    first = (first + stat_recv[0][:, :1]) / (2.0 * width)
    second = (second + stat_recv[1][:, :1]) / (2.0 * width)
    dx_ref[...] = (rstd_ref[:, :1] * (dn_buf[...] - first - xhat_ref[...] * second)).astype(BF16)
    gg_recv[col] = gg_send[...]
    for k in range(1, peers):
        gg_copy(k, (col + k) % peers).wait_recv()
    whole = gg_recv[0]
    for k in range(1, peers):
        whole = whole + gg_recv[k]
    dgain_ref[...] = whole
    stats.wait_send()
    for k in range(1, peers):
        gg_copy(k, col).wait_send()


def weight_gradient(left, right, tile, wide, first, count, into=None):
    tokens, height = left.shape
    columns = right.shape[1]

    def kernel(left_ref, right_ref, *rest):
        out_ref = rest[-1]
        turned = left_ref[...].T
        for at in range(0, columns, wide):
            out_ref[:, at:at + wide] = mm(turned, right_ref[:, at:at + wide]).astype(BF16)

    specs = [
        pl.BlockSpec((tokens, tile), lambda i: (0, i + first)),
        pl.BlockSpec((tokens, columns), lambda i: (0, 0)),
    ]
    more = () if into is None else (into,)
    rows = count * tile
    return pl.pallas_call(
        kernel,
        grid=(count,),
        out_shape=jax.ShapeDtypeStruct((height, columns), BF16),
        in_specs=specs + [pl.BlockSpec(memory_space=pl.ANY)] * len(more),
        out_specs=pl.BlockSpec((tile, columns), lambda i: (i + first, 0)),
        input_output_aliases={2: 0} if more else {},
        compiler_params=pltpu.CompilerParams(vmem_limit_bytes=58 * 2**20),
        cost_estimate=pl.CostEstimate(
            flops=2 * tokens * rows * columns,
            bytes_accessed=2 * (tokens * (rows + columns) + rows * columns),
            transcendentals=0,
        ),
    )(left, right, *more)


def pair_shards(layer_input, layer_norm_gain, w_qkv, w_out, out_grad):
    rows, width = layer_input.shape
    peers = lax.axis_size("col")
    chips = peers // 2
    tokens = rows * peers
    columns = w_qkv.shape[1]
    heads = columns // (3 * HS)
    own = heads // 2
    vmem = pl.BlockSpec(memory_space=pltpu.VMEM)
    hbm = pl.BlockSpec(memory_space=pl.ANY)
    dma = pltpu.SemaphoreType.DMA
    shape = jax.ShapeDtypeStruct
    normed, grad, context, dqkv, xhat, rstd, here, up, down, onward = pl.pallas_call(
        functools.partial(block_kernel, chips),
        out_shape=[
            shape((tokens, width), BF16),
            shape((tokens, width), BF16),
            shape((tokens, heads * HS), BF16),
            shape((tokens, columns), BF16),
            shape((rows, width), F32),
            shape((rows, HS), F32),
            shape((rows, width), F32),
            shape((rows, width), F32),
            shape((rows, width), F32),
            shape((rows, width), BF16),
        ],
        in_specs=[vmem, vmem, vmem, hbm, hbm],
        out_specs=[hbm] * 10,
        scratch_shapes=[
            pltpu.VMEM(w_qkv.shape, BF16),
            pltpu.VMEM(w_out.shape, BF16),
            pltpu.VMEM((tokens, width), BF16),
            pltpu.VMEM((tokens, width), BF16),
            pltpu.VMEM((rows, width), F32),
            pltpu.VMEM((rows, HS), F32),
            pltpu.VMEM((1, 2, rows, HS), F32),
            pltpu.VMEM((1, 2, rows, HS), F32),
            pltpu.VMEM((own, tokens, 3 * HS), BF16),
            pltpu.VMEM((own, tokens, 3 * HS), BF16),
            pltpu.VMEM((own, tokens, 3 * HS), BF16),
            pltpu.VMEM((own, tokens, tokens), F32),
            pltpu.VMEM((heads, tokens, HS), BF16),
            pltpu.VMEM((tokens, own * HS), BF16),
            pltpu.VMEM((tokens, own * HS), BF16),
            pltpu.VMEM((own, tokens, HS), BF16),
            pltpu.VMEM((tokens, columns), BF16),
            pltpu.VMEM((chips, rows, width), F32),
            pltpu.VMEM((chips, rows, width), BF16),
            pltpu.VMEM((chips, rows, width), BF16),
            pltpu.VMEM((rows, width), BF16),
            pltpu.VMEM((rows, width), BF16),
            pltpu.VMEM((2, rows, width), BF16),
            pltpu.VMEM((tokens, 3 * HS), F32),
            pltpu.VMEM((own, tokens, 3 * HS), F32),
            dma((2,)), dma((10,)), dma((heads,)), dma((1,)), dma((1,)),
            dma((2, chips)), dma((2, chips)), dma((2, chips)), dma((2, chips)), dma((2, chips)),
            dma((3, own)), dma((3, own)), dma((own,)), dma((own,)),
            dma((2,)), dma((2,)), dma((own,)), dma((own,)),
            dma((chips,)), dma((chips,)), dma((2,)), dma((2,)),
        ],
        compiler_params=pltpu.CompilerParams(
            collective_id=0, has_side_effects=True, vmem_limit_bytes=63 * 2**20
        ),
    )(layer_input, layer_norm_gain.reshape(1, width), out_grad, w_qkv, w_out)
    half = chips // 2
    both = range(2)
    rise = [(2 * z + c, 2 * z + 2 + c) for z in range(chips - 1) for c in both]
    fall = [(b, a) for a, b in rise]
    rise_first = [(2 * z + c, 2 * z + 2 + c) for z in range(half) for c in both]
    fall_first = [(2 * z + c, 2 * z - 2 + c) for z in range(half, chips) for c in both]
    got_up = lax.ppermute(onward, "col", rise_first)
    got_down = lax.ppermute(onward, "col", fall_first)
    tile = 512
    tiles = width // tile
    early = 2 * tiles // 3
    grad_wqkv = weight_gradient(normed, dqkv, tile, 3 * HS, 0, early)
    got_up, got_down, grad_wqkv = lax.optimization_barrier((got_up, got_down, grad_wqkv))
    next_up = (up + got_up.astype(F32)).astype(BF16)
    next_down = (down + got_down.astype(F32)).astype(BF16)
    from_below = lax.ppermute(next_up, "col", rise)
    from_above = lax.ppermute(next_down, "col", fall)
    grad_wqkv = weight_gradient(normed, dqkv, tile, 3 * HS, early, tiles - early, grad_wqkv)
    grad_wout = mm(context, grad, TN).astype(BF16)
    dx, dgain = pl.pallas_call(
        norm_kernel,
        out_shape=[shape((rows, width), BF16), shape((1, width), F32)],
        in_specs=[vmem] * 6,
        out_specs=[vmem] * 2,
        scratch_shapes=[
            pltpu.VMEM((rows, width), F32),
            pltpu.VMEM((2, rows, HS), F32),
            pltpu.VMEM((2, rows, HS), F32),
            pltpu.VMEM((1, width), F32),
            pltpu.VMEM((peers, 1, width), F32),
            dma((1,)), dma((1,)), dma((peers,)), dma((peers,)),
        ],
        compiler_params=pltpu.CompilerParams(
            collective_id=1, has_side_effects=True, vmem_limit_bytes=24 * 2**20
        ),
    )(here, from_below, from_above, xhat, rstd, layer_norm_gain.reshape(1, width))
    return dx, dgain.reshape(width), grad_wqkv, grad_wout


def choose(layer_input, layer_norm_gain, w_qkv, w_out, out_grad):
    paired = lax.axis_size("row") == 2 and lax.axis_size("col") == 8
    sized = layer_input.shape[1] % 1024 == 0 and layer_input.shape[0] == 32
    body = pair_shards if paired and sized and w_qkv.shape[1] == 18 * HS else shards
    return body(layer_input, layer_norm_gain, w_qkv, w_out, out_grad)


def solution(mesh):
    in_specs = (
        P(("dp", "col"), "row"),
        P("row"),
        P("row", "col"),
        P("col", "row"),
        P(("dp", "col"), "row"),
    )
    out_specs = (
        P(("dp", "col"), "row"),
        P(("dp", "row")),
        P(("dp", "row"), "col"),
        P(("dp", "col"), "row"),
    )
    return jax.shard_map(choose, mesh=mesh, in_specs=in_specs, out_specs=out_specs, check_vma=False)
```
